32 devices in a mesh: row: 8 (over y, x, core), col: 4 (over z).
Axes of the slice: x: 2, y: 2, z: 4, core: 2. Of those that a mesh axis runs over, the one named last changes fastest.
Arguments:
- tokens: bfloat16 [1280, 2048], P('row', 'col'), may hold values from -1600 to 1600, as said below
- norm_gain: float32 [2048], P('col'), may hold values from 0.1 to 1.9
- lengths: int32 [16], replicated, may hold values from 1 to 320, 1280 in all
- request_adapter: int32 [16], replicated, may hold values from 0 to 63
- routes: int32 [1280, 2], P('row'), may hold values from 0 to 7, all different within a row; in each aligned block of 160 rows (0 to 159, 160 to 319, ...) at most 60 rows name the same one
- route_weights: float32 [1280, 2], P('row'), may hold values from 0.2 to 1
- gate_weight: bfloat16 [8, 5632, 2048], P('row', 'col'), may hold values from -0.125 to 0.125
- up_weight: bfloat16 [8, 5632, 2048], P('row', 'col'), may hold values from -0.125 to 0.125
- down_weight: bfloat16 [8, 5632, 2048], P('row', None, 'col'), may hold values from -0.078125 to 0.078125
- adapter_down: bfloat16 [64, 2048, 16], P('row', 'col'), may hold values from -0.125 to 0.125
- adapter_up: bfloat16 [64, 16, 2048], P('row', None, 'col'), may hold values from -1.5 to 1.5
Outputs:
- mixed: bfloat16 [1280, 2048], P('row', 'col')
The draws below stay inside these ranges and needn't reach their ends.
Inputs may be any that keep to these rules, and one draw needn't show every extreme that they name: Feature scales differ over the features and token scales over the tokens. The lengths sum to 1280. `routes`: A token's two experts differ. Among the tokens of one index of row (aligned blocks of 160 tokens) no expert is named by more than 60 tokens, a bound that some block reaches.
All inputs are finite; a program needn't handle non-finite values.
Results may differ from the reference program's by a relative error of at most 0.008.
Values may be sent and summed in bfloat16 or wider, within the bound.
No kernel may reach another device: no remote copies, remote signals or barrier semaphores. Data moves between devices by JAX's collectives and lax.ppermute only.
A program may use at most 64 MiB of HBM per device.

```python
import math
import jax
import jax.numpy as jnp
import numpy as np
from jax import lax

D = 2048
FF = 5632
EXPERTS = 8
TOPK = 2
RANK = 16
ADAPTERS = 64
REQUESTS = 16
TOK_DEV = 160
TOKENS = 1280
UNITS = 8
UNIT_FF = 5632
CAP = 60
N_ROW = 8


def draw_tokens(key, part):
    first_key, second_key, third_key = jax.random.split(jax.random.fold_in(key, 11), 3)
    feature_scale = 10.0 ** (jnp.arange(D, dtype=jnp.float32) / D) * jnp.exp(jax.random.uniform(second_key, (D,), jnp.float32, -0.5, 0.5))
    base = jnp.clip(jax.random.normal(first_key, (TOKENS, D), jnp.float32), -6.0, 6.0)
    token_scale = jnp.exp(jax.random.uniform(third_key, (TOKENS, 1), jnp.float32, 0.0, math.log(10.0)))
    return (base * feature_scale[None, :] * token_scale).astype(jnp.bfloat16)


def set_ends(values, key, low, largest):
    place = [jax.random.randint(jax.random.fold_in(key, axis), (), 0, length) for axis, length in enumerate(values.shape)]
    widest = values.shape.index(max(values.shape))
    next_to = place[:widest] + [(place[widest] + 1) % values.shape[widest]] + place[widest + 1:]
    return values.at[tuple(place)].set(low).at[tuple(next_to)].set(largest)


def block_levels(rng, shape, pieces, least, top_value):
    level, own = 1.0, jax.random.fold_in(rng, 6)
    for axis_at, shards_of in pieces:
        heights = jnp.exp(jax.random.uniform(jax.random.fold_in(own, axis_at), (shards_of,), jnp.float32, least / len(pieces), top_value / len(pieces)))
        level = level * jnp.repeat(heights, shape[axis_at] // shards_of).reshape([-1 if axis == axis_at else 1 for axis in range(len(shape))])
    return level


def split_up(amount, total, bound, skew):
    loads = [(1 << 20) // math.isqrt(standing ** skew) + 1 for standing in range(2, amount + 1)]
    rest, counts = total - bound - (amount - 1), [1] * (amount - 1)
    while rest > 0:
        candidates = [i for i in range(amount - 1) if counts[i] < bound]
        pool, remaining = sum([loads[i] for i in candidates]), rest
        for i in candidates:
            extra = min(bound - counts[i], max(1, remaining * loads[i] // pool), rest)
            counts[i] = counts[i] + extra
            rest = rest - extra
    return np.array([bound] + counts)


def uneven_parts(rng, count, total, most, slope):
    if count == 2:
        one = jax.random.randint(rng, (), max(1, total - most), min(most, total - 1) + 1)
        return jnp.stack([one, total - one])
    tallies = jnp.asarray(split_up(count, total, most, slope), jnp.int32)
    couples = (count - 1) // 2
    donor, sink = tallies[1:1 + 2 * couples:2], tallies[2:2 + 2 * couples:2]
    room = jnp.minimum(donor - 1, most - sink)
    moved = jax.random.randint(jax.random.fold_in(rng, 1), (couples,), 0, 1 << 20) % (room + 1)
    tallies = tallies.at[1:1 + 2 * couples:2].set(donor - moved).at[2:2 + 2 * couples:2].set(sink + moved)
    return tallies[jax.random.permutation(jax.random.fold_in(rng, 2), count)]


def shared_out(own_key, own, number, rows, amount, top, bound, slope):
    sequence = jax.random.permutation(own_key, amount)
    heavy_load, usual = portions_of(amount, rows * top, bound, slope, True), portions_of(amount, rows * top, bound, slope, False)
    places = jnp.arange(amount)

    def named(tallies, offset_by):
        used = int((tallies > 0).sum())
        fixed = max(1, used // 4)
        passed = fixed + (places - fixed + offset_by * (used - fixed)) % max(1, amount - fixed)
        return jnp.zeros((amount,), jnp.int32).at[sequence[jnp.where(places < fixed, places, passed)]].set(jnp.asarray(tallies, jnp.int32))

    tallies = jnp.where(number % 4 == 0, named(heavy_load, number // 4), named(usual, number - number // 4 - 1))
    mixed = jax.random.permutation(jax.random.fold_in(own, 3), amount)
    source_of, receiver = mixed[0:amount // 2 * 2:2], mixed[1:amount // 2 * 2:2]
    margin = jnp.minimum(tallies[source_of] - 1, bound - tallies[receiver]) // 2
    margin = jnp.where((source_of == sequence[0]) | (receiver == sequence[0]) | (tallies[receiver] == 0), 0, jnp.maximum(margin, 0))
    passed = jax.random.randint(jax.random.fold_in(own, 4), (amount // 2,), 0, 1 << 20) % (margin + 1)
    tallies = tallies.at[source_of].add(-passed).at[receiver].add(passed)
    items = jnp.searchsorted(jnp.cumsum(tallies), jnp.arange(rows * top), side="right").astype(jnp.int32)
    listing = items.reshape(top, rows).T
    listing = listing[jax.random.permutation(jax.random.fold_in(own, 1), rows)]
    offset_by = jax.random.randint(jax.random.fold_in(own, 2), (rows, 1), 0, top)
    return jnp.take_along_axis(listing, (jnp.arange(top)[None, :] + offset_by) % top, axis=1)


def portions_of(amount, total, most, slope, full):
    portions = [(1 << 20) // math.isqrt(standing ** slope) + 1 for standing in range(1, amount + 1)]
    largest = most if full else min(most, max(-(-total // amount), total * portions[0] // sum(portions)))
    least = 1 if total - largest >= amount - 1 else 0
    given, spare = [largest] + [least] * (amount - 1), total - largest - least * (amount - 1)
    while spare > 0:
        free = [i for i in range(1, amount) if given[i] < largest] or [i for i in range(1, amount) if given[i] < most]
        pool, remaining = sum([portions[i] for i in free]), spare
        for i in free:
            addition = min(most - given[i], max(1, remaining * portions[i] // pool), spare)
            given[i] = given[i] + addition
            spare = spare - addition
    return np.array(given)


def scatter_about(stream_key, extent, deviation, reach, cuts=(), kind=jnp.bfloat16):
    values = jax.random.normal(stream_key, extent, jnp.float32) * deviation
    if len(cuts) > 0:
        values = block_levels(stream_key, extent, cuts, -0.22, 0.18) * values
    return jnp.clip(values, min=-reach, max=reach).astype(kind)


def setup_inputs(seed: int = 0) -> dict:
    key_of = jax.random.split(jax.random.key(seed), 12)
    tokens = draw_tokens(jax.random.fold_in(key_of[11], 71), 0)
    norm_gain = jnp.clip(1.0 + 0.18 * jax.random.normal(key_of[1], (D,), jnp.float32), 0.1, 1.9)
    lengths = uneven_parts(key_of[2], REQUESTS, TOKENS, TOKENS // 4, 2).astype(jnp.int32)
    request_adapter = set_ends(jax.random.randint(key_of[3], (REQUESTS,), 0, ADAPTERS), jax.random.fold_in(key_of[3], 1), 0, ADAPTERS - 1).astype(jnp.int32)
    routes_keys = jax.random.split(jax.random.fold_in(key_of[4], 1), TOKENS // TOK_DEV)
    routes_turns = jax.random.permutation(jax.random.fold_in(key_of[4], 3), TOKENS // TOK_DEV)
    routes = jax.vmap(lambda own, number: shared_out(jax.random.fold_in(key_of[4], 2), own, number, TOK_DEV, EXPERTS, TOPK, CAP, 2))(routes_keys, routes_turns).reshape((TOKENS, TOPK))
    route_weights = jnp.clip(0.2 + 0.8 * jax.random.uniform(key_of[5], (TOKENS, TOPK), jnp.float32) ** block_levels(key_of[5], (TOKENS, TOPK), ((0, 8),), -0.2, 0.2), 0.2, 1.0)
    gate_weight = scatter_about(key_of[6], (UNITS, UNIT_FF, D), D ** -0.5, 0.125, ((0, 8), (1, 4)))
    up_weight = scatter_about(key_of[7], (UNITS, UNIT_FF, D), D ** -0.5, 0.125, ((0, 8), (1, 4)))
    down_weight = scatter_about(key_of[8], (UNITS, UNIT_FF, D), FF ** -0.5, 0.078125, ((0, 8), (2, 4)))
    adapter_down = scatter_about(key_of[9], (ADAPTERS, D, RANK), D ** -0.5, 0.125, ((0, 8), (1, 4)))
    adapter_up = scatter_about(key_of[10], (ADAPTERS, RANK, D), RANK ** -0.5, 1.5, ((0, 8), (2, 4)))
    return dict(tokens=tokens, norm_gain=norm_gain, lengths=lengths, request_adapter=request_adapter, routes=routes, route_weights=route_weights, gate_weight=gate_weight, up_weight=up_weight, down_weight=down_weight, adapter_down=adapter_down, adapter_up=adapter_up)


def reference(tokens, norm_gain, lengths, request_adapter, routes, route_weights, gate_weight, up_weight, down_weight, adapter_down, adapter_up):
    splits = N_ROW // EXPERTS
    widened = tokens.astype(jnp.float32)
    mean_square = lax.optimization_barrier(jnp.mean(widened * widened, axis=1, keepdims=True))
    normed = (widened * lax.rsqrt(mean_square + 1e-06) * norm_gain[None, :]).astype(jnp.bfloat16)
    req_ends = jnp.cumsum(lengths)
    position = jnp.arange(TOKENS, dtype=jnp.int32)
    request = lax.optimization_barrier(jnp.sum((position[:, None] >= req_ends[None, :]).astype(jnp.int32), axis=1))
    adapter = request_adapter[request]
    select = (adapter[:, None] == jnp.arange(ADAPTERS, dtype=jnp.int32)[None, :]).astype(jnp.float32)
    down_matrix = jnp.transpose(adapter_down, (1, 0, 2)).reshape(D, ADAPTERS * RANK)
    projected = jnp.dot(normed, down_matrix, preferred_element_type=jnp.float32).reshape(TOKENS, ADAPTERS, RANK)
    low_rank = lax.optimization_barrier(jnp.sum(projected * select[:, :, None], axis=1)).astype(jnp.bfloat16)
    expanded = (select.astype(jnp.bfloat16)[:, :, None] * low_rank[:, None, :]).reshape(TOKENS, ADAPTERS * RANK)
    branch = jnp.dot(expanded, adapter_up.reshape(ADAPTERS * RANK, D), preferred_element_type=jnp.float32)
    gate_full = jnp.transpose(gate_weight.reshape(EXPERTS, splits, UNIT_FF, D), (0, 3, 1, 2)).reshape(EXPERTS, D, FF)
    up_full = jnp.transpose(up_weight.reshape(EXPERTS, splits, UNIT_FF, D), (0, 3, 1, 2)).reshape(EXPERTS, D, FF)
    down_blocks = down_weight.reshape(EXPERTS, splits, UNIT_FF, D)
    matches = (routes[:, :, None] == jnp.arange(EXPERTS, dtype=jnp.int32)[None, None, :]).astype(jnp.float32)
    combine = lax.optimization_barrier(jnp.sum(matches * route_weights[:, :, None], axis=1))

    def scan_step(running, stacked):
        gate_mat, up_mat, down_mat, weight_col = stacked
        gate_sum = jnp.dot(normed, gate_mat, preferred_element_type=jnp.float32)
        up_sum = jnp.dot(normed, up_mat, preferred_element_type=jnp.float32)
        hidden = (jax.nn.silu(gate_sum) * up_sum).astype(jnp.bfloat16)
        hidden_blocks = hidden.reshape(TOKENS, splits, UNIT_FF).astype(jnp.float32)
        block_out = jnp.einsum('tqf,qfd->tqd', hidden_blocks, down_mat.astype(jnp.float32)).astype(jnp.bfloat16)
        expert_out = lax.optimization_barrier(jnp.sum(block_out.astype(jnp.float32), axis=1))
        return (running + weight_col[:, None] * expert_out, None)
    moe_sum, unused = lax.scan(scan_step, jnp.zeros((TOKENS, D), jnp.float32), (gate_full, up_full, down_blocks, combine.T))
    return (moe_sum + branch).astype(jnp.bfloat16)
```

```python
import jax
import jax.numpy as jnp
from jax import lax
from jax.sharding import PartitionSpec as P

D = 2048
EXPERTS = 8
TOPK = 2
RANK = 16
CAP = 60
GAIN_ROWS = 16
LOW_ROWS = 8
LOW_STRIDE = 256


def contract_last(left, right):
    return lax.dot_general(
        left, right, (((1,), (1,)), ((), ())), preferred_element_type=jnp.float32
    )


def col_shift(value, by):
    size = lax.axis_size("col")
    return lax.ppermute(value, "col", [(i, (i + by) % size) for i in range(size)])


def row_xor(value, by):
    return lax.ppermute(value, "row", [(i, i ^ by) for i in range(lax.axis_size("row"))])


def ring_gather(value):
    size = lax.axis_size("col")
    rows = value.shape[0]
    half = -(-rows // 16) * 8
    found = [(0, 0, value)]
    from_left, from_right = value, value
    for hop in range(1, (size + 1) // 2):
        from_left, from_right = col_shift(from_left, 1), col_shift(from_right, -1)
        found += [(hop, 0, from_left), (-hop, 0, from_right)]
    if size % 2 == 0:
        found += [
            (size // 2, 0, col_shift(from_left[:half], 1)),
            (-size // 2, half, col_shift(from_right[half:], -1)),
        ]
    return found


def lay_out(pieces, rows, width):
    size = lax.axis_size("col")
    here = lax.axis_index("col")
    whole = jnp.zeros((rows, size * width), pieces[0][2].dtype)
    for distance, first, block in pieces:
        source = lax.rem(here - distance + size, size)
        whole = lax.dynamic_update_slice(whole, block, (first, source * width))
    return whole


def split_float(value, parts):
    pieces = []
    for _ in range(parts):
        piece = value.astype(jnp.bfloat16)
        pieces.append(piece)
        value = value - piece.astype(jnp.float32)
    return pieces


def body(
    tokens,
    norm_gain,
    lengths,
    request_adapter,
    routes,
    route_weights,
    gate_weight,
    up_weight,
    down_weight,
    adapter_down,
    adapter_up,
):
    tok_rows, width_part = tokens.shape
    rows_axis, cols_axis = lax.axis_size("row"), lax.axis_size("col")
    row_at, col_at = lax.axis_index("row"), lax.axis_index("col")
    splits = rows_axis // EXPERTS
    chips = rows_axis // 2
    unit_gate, unit_up, unit_down = gate_weight[0], up_weight[0], down_weight[0]
    hidden_part = unit_gate.shape[0]

    down_all, up_all = (
        lax.all_gather(adapter_down, "row", axis=0, tiled=True),
        lax.all_gather(adapter_up, "row", axis=0, tiled=True),
    )

    gain_parts = jnp.stack(split_float(norm_gain, 3))
    sent = jnp.concatenate(
        [tokens, jnp.pad(gain_parts, ((0, GAIN_ROWS - 3), (0, 0)))], axis=0
    )
    gathered_rows = sent.shape[0]
    features = lay_out(ring_gather(sent), gathered_rows, width_part)

    assigned = routes.reshape(-1)
    assign_count = assigned.shape[0]
    expert_hot = (assigned[:, None] == jnp.arange(EXPERTS, dtype=jnp.int32)[None, :]).astype(
        jnp.bfloat16
    )
    earlier = (
        jnp.arange(assign_count, dtype=jnp.int32)[:, None]
        > jnp.arange(assign_count, dtype=jnp.int32)[None, :]
    ).astype(jnp.bfloat16)
    before = jnp.dot(earlier, expert_hot, preferred_element_type=jnp.float32)
    slot_index = jnp.sum(before * expert_hot.astype(jnp.float32), axis=1).astype(jnp.int32)
    place = jnp.arange(chips * 2 * CAP, dtype=jnp.int32)
    target = row_at ^ (place // CAP)
    wanted = (target // splits) * CAP + place % CAP
    placed_at = assigned * CAP + slot_index
    placing = (wanted[:, None] == placed_at[None, :]).astype(jnp.bfloat16)
    placing_tokens = jnp.sum(placing.reshape(-1, tok_rows, TOPK), axis=2)

    widened = features[:tok_rows].astype(jnp.float32)
    gain = jnp.sum(features[tok_rows : tok_rows + 3].astype(jnp.float32), axis=0)
    scale = lax.rsqrt(jnp.mean(widened * widened, axis=1, keepdims=True) + 1e-06)
    normed = (widened * scale * gain[None, :]).astype(jnp.bfloat16)
    outgoing = jnp.dot(placing_tokens, normed, preferred_element_type=jnp.float32).astype(
        jnp.bfloat16
    ).reshape(chips, 2, CAP, D)
    here_half, there_half = outgoing[:, 0], outgoing[:, 1]
    partner_half = row_xor(there_half, 1)

    own = lax.dynamic_slice(normed, (0, col_at * width_part), (tok_rows, width_part))
    req_ends = jnp.cumsum(lengths)
    position = row_at * tok_rows + jnp.arange(tok_rows, dtype=jnp.int32)
    request = jnp.sum((position[:, None] >= req_ends[None, :]).astype(jnp.int32), axis=1)
    request_hot = request[:, None] == jnp.arange(lengths.shape[0], dtype=jnp.int32)[None, :]
    adapter = jnp.sum(jnp.where(request_hot, request_adapter[None, :], 0), axis=1)
    adapter_count = adapter_down.shape[0] * rows_axis
    select = (adapter[:, None] == jnp.arange(adapter_count, dtype=jnp.int32)[None, :]).astype(
        jnp.float32
    )
    down_matrix = jnp.transpose(down_all, (1, 0, 2)).reshape(width_part, adapter_count * RANK)
    projected = jnp.dot(own, down_matrix, preferred_element_type=jnp.float32).reshape(
        tok_rows, adapter_count, RANK
    )
    partial_low = jnp.sum(projected * select[:, :, None], axis=1)

    groups = [[0], list(range(1, chips - 1)), [chips - 1]]
    low_group = 1
    low_sum = None
    returned = [None] * chips
    for number, offsets in enumerate(groups):
        blocks = []
        for offset in offsets:
            pair = jnp.concatenate([here_half[offset], partner_half[offset]], axis=0)
            blocks.append(pair if offset == 0 else row_xor(pair, 2 * offset))
        arrived = jnp.concatenate(blocks, axis=0)
        gate_sum = contract_last(arrived, unit_gate)
        up_sum = contract_last(arrived, unit_up)
        hidden = (jax.nn.silu(gate_sum) * up_sum).astype(jnp.bfloat16)
        count = hidden.shape[0]
        if number == low_group:
            high, low = split_float(partial_low, 2)
            flat = jnp.concatenate([high, low], axis=1).reshape(-1)
            extra = -(-flat.shape[0] // hidden_part)
            extra_rows = -(-extra // 8) * 8
            flat = jnp.pad(flat, (0, extra_rows * hidden_part - flat.shape[0]))
            hidden = jnp.concatenate([hidden, flat.reshape(extra_rows, hidden_part)], axis=0)
        pieces = ring_gather(hidden)
        whole = lay_out(pieces, hidden.shape[0], hidden_part)
        if number == low_group:
            rest = whole[count:].reshape(extra_rows, cols_axis, hidden_part)
            rest = jnp.transpose(rest, (1, 0, 2)).reshape(cols_axis, -1)
            rest = rest[:, : tok_rows * 2 * RANK].reshape(cols_axis, tok_rows, 2, RANK)
            low_sum = jnp.sum(rest.astype(jnp.float32), axis=(0, 2))
        block_out = jnp.dot(
            whole[:count], unit_down, preferred_element_type=jnp.float32
        ).astype(jnp.bfloat16)
        for index, offset in enumerate(offsets):
            piece = block_out[index * 2 * CAP : (index + 1) * 2 * CAP]
            returned[offset] = piece if offset == 0 else row_xor(piece, 2 * offset)

    low_rank = low_sum.astype(jnp.bfloat16)
    expanded = (select.astype(jnp.bfloat16)[:, :, None] * low_rank[:, None, :]).reshape(
        tok_rows, adapter_count * RANK
    )
    branch = jnp.dot(
        expanded,
        up_all.reshape(adapter_count * RANK, width_part),
        preferred_element_type=jnp.float32,
    )
    back = jnp.stack(returned).reshape(chips, 2, CAP, width_part)
    back_partner = row_xor(back[:, 1], 1)
    back = jnp.stack([back[:, 0], back_partner], axis=1).reshape(-1, width_part)
    taken = lax.dot_general(
        placing, back, (((0,), (0,)), ((), ())), preferred_element_type=jnp.float32
    ).reshape(tok_rows, TOPK, width_part)
    weighted = jnp.sum(taken * route_weights[:, :, None], axis=1)
    return (weighted + branch).astype(jnp.bfloat16)


def solution(mesh):
    in_specs = (
        P("row", "col"),
        P("col"),
        P(),
        P(),
        P("row", None),
        P("row", None),
        P("row", "col", None),
        P("row", "col", None),
        P("row", None, "col"),
        P("row", "col", None),
        P("row", None, "col"),
    )
    out_specs = P("row", "col")
    return jax.shard_map(body, mesh=mesh, in_specs=in_specs, out_specs=out_specs, check_vma=False)
```

```python
import jax
import jax.numpy as jnp
from jax import lax
from jax.sharding import PartitionSpec as P

D = 2048
EXPERTS = 8
TOPK = 2
RANK = 16
CAP = 60
GAIN_ROWS = 16
SLOTS = 64
AHEAD = (0, 1, 0)


def contract_last(left, right):
    return lax.dot_general(
        left, right, (((1,), (1,)), ((), ())), preferred_element_type=jnp.float32
    )


def col_shift(value, by):
    size = lax.axis_size("col")
    return lax.ppermute(value, "col", [(i, (i + by) % size) for i in range(size)])


def row_xor(value, by):
    return lax.ppermute(value, "row", [(i, i ^ by) for i in range(lax.axis_size("row"))])


def along(value, pairs):
    return lax.ppermute(value, "col", pairs)


BESIDE = [(0, 1), (1, 0), (2, 3), (3, 2)]
MIRROR = [(0, 3), (1, 2), (2, 1), (3, 0)]
OVER = [(0, 2), (3, 1)]
OUTWARD = [(1, 0), (2, 3)]


def first_hops(value):
    return along(value, MIRROR), along(value, BESIDE), along(value, OVER)


def in_line(value, mirror, beside, over, passed):
    here = lax.axis_index("col")
    return side_by_side(
        value, [(here ^ 1, 0, beside), (here ^ 3, 0, mirror), (here ^ 2, 0, over + passed)]
    )


def ring_gather(value):
    size = lax.axis_size("col")
    here = lax.axis_index("col")
    rows = value.shape[0]
    half = -(-rows // 16) * 8
    found = []
    from_left, from_right = value, value
    for hop in range(1, (size + 1) // 2):
        from_left, from_right = col_shift(from_left, 1), col_shift(from_right, -1)
        found += [
            (lax.rem(here + size - hop, size), 0, from_left),
            (lax.rem(here + hop, size), 0, from_right),
        ]
    if size % 2 == 0:
        facing = lax.rem(here + size // 2, size)
        found += [
            (facing, 0, col_shift(from_left[:half], 1)),
            (facing, half, col_shift(from_right[half:], -1)),
        ]
    return found


def side_by_side(value, others):
    rows, width = value.shape
    whole = jnp.zeros((rows, lax.axis_size("col") * width), value.dtype)
    for sender, first, block in [(lax.axis_index("col"), 0, value)] + others:
        whole = lax.dynamic_update_slice(whole, block, (first, sender * width))
    return whole


def col_sum(value):
    size = lax.axis_size("col")
    total = value
    for by in range(1, size):
        total = total + lax.ppermute(value, "col", [(i, i ^ by) for i in range(size)])
    return total


def row_gather_chips(value):
    size = lax.axis_size("row")
    return jnp.stack([value] + [row_xor(value, by) for by in range(2, size, 2)])


def both_cores(stacked):
    both = jnp.stack([stacked, row_xor(stacked, 1)], axis=1)
    return both.reshape((lax.axis_size("row"),) + stacked.shape[1:])


def normalised(features, rows):
    widened = features[:rows].astype(jnp.float32)
    gain = jnp.sum(features[rows : rows + 3].astype(jnp.float32), axis=0)
    scale = lax.rsqrt(jnp.mean(widened * widened, axis=1, keepdims=True) + 1e-06)
    return (widened * scale * gain[None, :]).astype(jnp.bfloat16)


def after(value, *others):
    return lax.optimization_barrier((value,) + others)[0]


def split_float(value, parts):
    pieces = []
    for _ in range(parts):
        piece = lax.reduce_precision(value, 8, 7)
        pieces.append(piece.astype(jnp.bfloat16))
        value = value - piece
    return pieces


def body(
    tokens,
    norm_gain,
    lengths,
    request_adapter,
    routes,
    route_weights,
    gate_weight,
    up_weight,
    down_weight,
    adapter_down,
    adapter_up,
):
    tok_rows, width_part = tokens.shape
    rows_axis, cols_axis = lax.axis_size("row"), lax.axis_size("col")
    row_at, col_at = lax.axis_index("row"), lax.axis_index("col")
    splits = rows_axis // EXPERTS
    chips = rows_axis // 2
    unit_gate, unit_up, unit_down = gate_weight[0], up_weight[0], down_weight[0]
    hidden_part = unit_gate.shape[0]
    line = cols_axis == 4

    gain_parts = jnp.stack(split_float(norm_gain, 3))
    sent = jnp.concatenate(
        [tokens, jnp.pad(gain_parts, ((0, GAIN_ROWS - 3), (0, 0)))], axis=0
    )
    if line:
        mirror, beside, over = first_hops(sent)
        features = in_line(sent, mirror, beside, over, along(mirror, OUTWARD))
    else:
        features = side_by_side(sent, ring_gather(sent))
    normed = normalised(features, tok_rows)

    assigned = routes.reshape(-1)
    assign_count = assigned.shape[0]
    expert_hot = (assigned[:, None] == jnp.arange(EXPERTS, dtype=jnp.int32)[None, :]).astype(
        jnp.bfloat16
    )
    earlier = (
        jnp.arange(assign_count, dtype=jnp.int32)[:, None]
        > jnp.arange(assign_count, dtype=jnp.int32)[None, :]
    ).astype(jnp.bfloat16)
    before = jnp.dot(earlier, expert_hot, preferred_element_type=jnp.float32)
    slot_index = jnp.sum(before * expert_hot.astype(jnp.float32), axis=1).astype(jnp.int32)
    placed_at = assigned * SLOTS + slot_index

    def placing(core, slots):
        place = jnp.arange(chips * slots, dtype=jnp.int32)
        target = row_at ^ (place // slots * 2 + core)
        wanted = (target // splits) * SLOTS + place % slots
        return (wanted[:, None] == placed_at[None, :]).astype(jnp.bfloat16)

    def outgoing(core):
        of_token = jnp.sum(placing(core, SLOTS).reshape(-1, tok_rows, TOPK), axis=2)
        placed = jnp.dot(of_token, normed, preferred_element_type=jnp.float32)
        return placed.astype(jnp.bfloat16).reshape(chips, SLOTS, D)

    partner_half = row_xor(outgoing(1), 1)
    here_half = outgoing(0)

    local_adapters = adapter_down.shape[0]
    mine = jnp.concatenate([jnp.transpose(adapter_down, (0, 2, 1)), adapter_up], axis=0)
    mine = mine.reshape(2 * local_adapters * RANK, width_part)
    by_chip = row_gather_chips(mine)
    groups = [[0], list(range(1, chips - 1)), [chips - 1]]
    pairs = [
        jnp.concatenate([here_half[offset], partner_half[offset]], axis=0)
        for offset in range(chips)
    ]
    for offset in range(1, chips):
        pair = after(pairs[offset], pairs[1]) if offset == chips - 1 else pairs[offset]
        pairs[offset] = row_xor(pair, 2 * offset)

    def hidden_of(offsets, *earlier):
        arrived = jnp.concatenate(
            [
                pairs[offset][first : first + CAP]
                for offset in offsets
                for first in (0, SLOTS)
            ],
            axis=0,
        )
        arrived = after(arrived, *earlier)
        gate_sum = contract_last(arrived, unit_gate)
        up_sum = contract_last(arrived, unit_up)
        return (jax.nn.silu(gate_sum) * up_sum).astype(jnp.bfloat16)

    hidden, hops = [], []
    for offsets in groups:
        hidden.append(hidden_of(offsets))
        hops.append(first_hops(hidden[-1]) if line else ring_gather(hidden[-1]))

    factors = both_cores(after(by_chip, hidden[0]))
    factors = factors.reshape(rows_axis, 2, local_adapters * RANK, width_part)
    down_rows = factors[:, 0].reshape(-1, width_part)
    up_rows = factors[:, 1].reshape(-1, width_part)
    own = lax.dynamic_slice(after(normed, hidden[min(1, len(groups) - 1)]), (0, col_at * width_part), (tok_rows, width_part))
    req_ends = jnp.cumsum(lengths)
    position = row_at * tok_rows + jnp.arange(tok_rows, dtype=jnp.int32)
    request = jnp.sum((position[:, None] >= req_ends[None, :]).astype(jnp.int32), axis=1)
    request_hot = request[:, None] == jnp.arange(lengths.shape[0], dtype=jnp.int32)[None, :]
    adapter = jnp.sum(jnp.where(request_hot, request_adapter[None, :], 0), axis=1)
    adapter_count = local_adapters * rows_axis
    order = jnp.arange(adapter_count, dtype=jnp.int32)
    held = (row_at ^ (order // local_adapters)) * local_adapters + order % local_adapters
    select = (adapter[:, None] == held[None, :]).astype(jnp.float32)
    projected = contract_last(own, down_rows).reshape(tok_rows, adapter_count, RANK)
    partial_low = jnp.sum(projected * select[:, :, None], axis=1)

    low_sum = col_sum(partial_low)
    low_rank = low_sum.astype(jnp.bfloat16)
    expanded = (select.astype(jnp.bfloat16)[:, :, None] * low_rank[:, None, :]).reshape(
        tok_rows, adapter_count * RANK
    )
    branch = jnp.dot(expanded, up_rows, preferred_element_type=jnp.float32)

    def returns(numbers, whole):
        block_out = jnp.dot(whole, unit_down, preferred_element_type=jnp.float32).astype(
            jnp.bfloat16
        )
        offsets = [offset for number in numbers for offset in groups[number]]
        for index, offset in enumerate(offsets):
            piece = block_out[index * 2 * CAP : (index + 1) * 2 * CAP]
            returned[offset] = piece if offset == 0 else row_xor(piece, 2 * offset)
        return block_out

    returned = [None] * chips
    done = branch
    for number, value in enumerate(hidden):
        if line:
            mirror, beside, over = hops[number]
            passed = along(after(mirror, hidden[min(number + AHEAD[number], 2)]), OUTWARD)
            beside, over = after(beside, mirror), after(over, mirror)
            whole = in_line(value, mirror, beside, over, passed)
        else:
            whole = side_by_side(value, hops[number])
        done = returns([number], after(whole, done, hidden[-1]))
    back = jnp.stack(returned)
    taken = sum(
        lax.dot_general(
            placing(core, CAP),
            part.reshape(-1, width_part),
            (((0,), (0,)), ((), ())),
            preferred_element_type=jnp.float32,
        )
        for core, part in ((0, back[:, :CAP]), (1, row_xor(back[:, CAP:], 1)))
    ).reshape(tok_rows, TOPK, width_part)
    weighted = jnp.sum(taken * route_weights[:, :, None], axis=1)
    return (weighted + branch).astype(jnp.bfloat16)


def solution(mesh):
    in_specs = (
        P("row", "col"),
        P("col"),
        P(),
        P(),
        P("row", None),
        P("row", None),
        P("row", "col", None),
        P("row", "col", None),
        P("row", None, "col"),
        P("row", "col", None),
        P("row", None, "col"),
    )
    out_specs = P("row", "col")
    return jax.shard_map(body, mesh=mesh, in_specs=in_specs, out_specs=out_specs, check_vma=False)
```

```python
import jax
import jax.numpy as jnp
from jax import lax
from jax.sharding import PartitionSpec as P

D = 2048
EXPERTS = 8
TOPK = 2
RANK = 16
CAP = 60
GAIN_ROWS = 8
LOW_STRIDE = 256
SLOTS = 64


def contract_last(left, right):
    return lax.dot_general(
        left, right, (((1,), (1,)), ((), ())), preferred_element_type=jnp.float32
    )


def col_shift(value, by):
    size = lax.axis_size("col")
    return lax.ppermute(value, "col", [(i, (i + by) % size) for i in range(size)])


def row_xor(value, by):
    return lax.ppermute(value, "row", [(i, i ^ by) for i in range(lax.axis_size("row"))])


def along(value, pairs):
    return lax.ppermute(value, "col", pairs)


BESIDE = [(0, 1), (1, 0), (2, 3), (3, 2)]
MIRROR = [(0, 3), (1, 2), (2, 1), (3, 0)]
OVER = [(0, 2), (3, 1)]
FACING = [(0, 2), (1, 3), (2, 0), (3, 1)]
OUTWARD = [(1, 0), (2, 3)]


def first_hops(value, whole):
    return (
        along(value, MIRROR),
        along(value, BESIDE),
        along(value, FACING if whole else OVER),
    )


def in_line(value, mirror, beside, facing):
    here = lax.axis_index("col")
    return side_by_side(
        value, [(here ^ 1, 0, beside), (here ^ 3, 0, mirror), (here ^ 2, 0, facing)]
    )


def ring_gather(value):
    size = lax.axis_size("col")
    here = lax.axis_index("col")
    rows = value.shape[0]
    half = -(-rows // 16) * 8
    found = []
    from_left, from_right = value, value
    for hop in range(1, (size + 1) // 2):
        from_left, from_right = col_shift(from_left, 1), col_shift(from_right, -1)
        found += [
            (lax.rem(here + size - hop, size), 0, from_left),
            (lax.rem(here + hop, size), 0, from_right),
        ]
    if size % 2 == 0:
        facing = lax.rem(here + size // 2, size)
        found += [
            (facing, 0, col_shift(from_left[:half], 1)),
            (facing, half, col_shift(from_right[half:], -1)),
        ]
    return found


def side_by_side(value, others):
    rows, width = value.shape
    whole = jnp.zeros((rows, lax.axis_size("col") * width), value.dtype)
    for sender, first, block in [(lax.axis_index("col"), 0, value)] + others:
        whole = lax.dynamic_update_slice(whole, block, (first, sender * width))
    return whole


def col_sum(value):
    size = lax.axis_size("col")
    total = value
    for by in range(1, size):
        total = total + lax.ppermute(value, "col", [(i, i ^ by) for i in range(size)])
    return total


def both_cores(stacked):
    both = jnp.stack([stacked, row_xor(stacked, 1)], axis=1)
    return both.reshape((lax.axis_size("row"),) + stacked.shape[1:])


def normalised(features, rows):
    widened = features[:rows].astype(jnp.float32)
    gain = jnp.sum(features[rows : rows + 3].astype(jnp.float32), axis=0)
    scale = lax.rsqrt(jnp.mean(widened * widened, axis=1, keepdims=True) + 1e-06)
    return (widened * scale * gain[None, :]).astype(jnp.bfloat16)


def tie(*values):
    return lax.optimization_barrier(values)


def split_float(value, parts):
    pieces = []
    for _ in range(parts):
        piece = lax.reduce_precision(value, 8, 7)
        pieces.append(piece.astype(jnp.bfloat16))
        value = value - piece
    return pieces


def body(
    tokens,
    norm_gain,
    lengths,
    request_adapter,
    routes,
    route_weights,
    gate_weight,
    up_weight,
    down_weight,
    adapter_down,
    adapter_up,
):
    tok_rows, width_part = tokens.shape
    rows_axis, cols_axis = lax.axis_size("row"), lax.axis_size("col")
    row_at, col_at = lax.axis_index("row"), lax.axis_index("col")
    splits = rows_axis // EXPERTS
    chips = rows_axis // 2
    unit_gate, unit_up, unit_down = gate_weight[0], up_weight[0], down_weight[0]
    hidden_part = unit_gate.shape[0]
    line = cols_axis == 4

    gain_parts = jnp.stack(split_float(norm_gain, 3))
    sent = jnp.concatenate(
        [tokens, jnp.pad(gain_parts, ((0, GAIN_ROWS - 3), (0, 0)))], axis=0
    )
    hops = first_hops(sent, True) if line else ring_gather(sent)

    local_adapters = adapter_down.shape[0]
    mine = jnp.concatenate([jnp.transpose(adapter_down, (0, 2, 1)), adapter_up], axis=0)
    mine = mine.reshape(2 * local_adapters * RANK, width_part)
    by_chip = [mine] + [row_xor(mine, by) for by in range(2, rows_axis, 2)]
    assigned = routes.reshape(-1)
    assign_count = assigned.shape[0]
    expert_hot = (assigned[:, None] == jnp.arange(EXPERTS, dtype=jnp.int32)[None, :]).astype(
        jnp.bfloat16
    )
    earlier = (
        jnp.arange(assign_count, dtype=jnp.int32)[:, None]
        > jnp.arange(assign_count, dtype=jnp.int32)[None, :]
    ).astype(jnp.bfloat16)
    before = jnp.dot(earlier, expert_hot, preferred_element_type=jnp.float32)
    slot_index = jnp.sum(before * expert_hot.astype(jnp.float32), axis=1).astype(jnp.int32)
    placed_at = assigned * SLOTS + slot_index

    def placing(core, slots):
        place = jnp.arange(chips * slots, dtype=jnp.int32)
        target = row_at ^ (place // slots * 2 + core)
        wanted = (target // splits) * SLOTS + place % slots
        return (wanted[:, None] == placed_at[None, :]).astype(jnp.bfloat16)

    of_token = [
        jnp.sum(placing(core, SLOTS).reshape(-1, tok_rows, TOPK), axis=2) for core in (0, 1)
    ]
    if line:
        hops, of_token = tie(hops, of_token)
    features = in_line(sent, *hops) if line else side_by_side(sent, hops)
    normed, *by_chip = tie(normalised(features, tok_rows), *by_chip)

    def outgoing(core):
        placed = jnp.dot(of_token[core], normed, preferred_element_type=jnp.float32)
        return placed.astype(jnp.bfloat16).reshape(chips, SLOTS, D)

    partner_half = row_xor(outgoing(1), 1)
    here_half = outgoing(0)

    groups = [[0], list(range(1, chips - 1)), [chips - 1]]
    pairs = [
        jnp.concatenate([here_half[offset], partner_half[offset]], axis=0)
        for offset in range(chips)
    ]
    for offset in range(1, chips):
        if offset == chips - 1:
            pairs[1:] = tie(*pairs[1:])
        pairs[offset] = row_xor(pairs[offset], 2 * offset)

    def hidden_of(offsets, earlier):
        arrived = jnp.concatenate(
            [
                pairs[offset][first : first + CAP]
                for offset in offsets
                for first in (0, SLOTS)
            ],
            axis=0,
        )
        arrived, *earlier = tie(arrived, *earlier)
        gate_sum = contract_last(arrived, unit_gate)
        up_sum = contract_last(arrived, unit_up)
        value = (jax.nn.silu(gate_sum) * up_sum).astype(jnp.bfloat16)
        return value, earlier

    def first_of(value, whole):
        return list(first_hops(value, whole)) if line else ring_gather(value)

    value, _ = hidden_of(groups[0], [])
    hidden, hops = [value], [first_of(value, False)]

    hidden[0], pairs[1:-1], by_chip = tie(hidden[0], pairs[1:-1], by_chip)
    factors = both_cores(jnp.stack(by_chip))
    factors = factors.reshape(rows_axis, 2, local_adapters * RANK, width_part)
    down_rows = factors[:, 0].reshape(-1, width_part)
    up_rows = factors[:, 1].reshape(-1, width_part)
    normed, pairs[1:-1] = tie(normed, pairs[1:-1])
    own = lax.dynamic_slice(normed, (0, col_at * width_part), (tok_rows, width_part))
    req_ends = jnp.cumsum(lengths)
    position = row_at * tok_rows + jnp.arange(tok_rows, dtype=jnp.int32)
    request = jnp.sum((position[None, :] >= req_ends[:, None]).astype(jnp.int32), axis=0)
    request_hot = request[None, :] == jnp.arange(lengths.shape[0], dtype=jnp.int32)[:, None]
    adapter = jnp.sum(jnp.where(request_hot, request_adapter[:, None], 0), axis=0)
    adapter_count = local_adapters * rows_axis
    order = jnp.arange(adapter_count, dtype=jnp.int32)
    held = (row_at ^ (order // local_adapters)) * local_adapters + order % local_adapters
    select = held[:, None] == adapter[None, :]
    projected = contract_last(down_rows, own).reshape(adapter_count, RANK, tok_rows)
    partial_low = jnp.sum(jnp.where(select[:, None, :], projected, 0.0), axis=0)
    extra = jnp.zeros((0, hidden_part), jnp.bfloat16)
    if line:
        pieces = [piece[at : at + 8] for piece in split_float(partial_low, 2) for at in (0, 8)]
        spare = (0, LOW_STRIDE - tok_rows)
        extra = jnp.concatenate([jnp.pad(piece, ((0, 0), spare)) for piece in pieces], axis=1)
        extra = jnp.pad(extra, ((0, 0), (0, hidden_part - extra.shape[1])))

    passed = along(hops[0][0], OUTWARD) if line else None
    value, (extra, *hops[0][:1]) = hidden_of(groups[1], [extra] + hops[0][:1])
    hidden.append(jnp.concatenate([value, extra], axis=0))
    hops.append(first_of(hidden[1], False))
    earlier = hops[0][1:] + [passed] if line else []
    pairs[-1], hidden[1] = tie(pairs[-1], hidden[1])
    value, (hidden[1], *earlier) = hidden_of(groups[2], [hidden[1]] + earlier)
    hidden.append(value)
    hops.append(first_of(value, True))
    if line:
        beside, over, passed = earlier
        hops[0] = [hops[0][0], beside, over + passed]

    def whole_of(number):
        return (in_line if line else side_by_side)(
            hidden[number], *(hops[number] if line else [hops[number]])
        )

    def block_sum(whole):
        return jnp.dot(whole, unit_down, preferred_element_type=jnp.float32)

    late_weights, hidden[2] = tie(route_weights, hidden[2])

    def weights_at(core):
        place = jnp.arange(chips * CAP, dtype=jnp.int32)
        target = row_at ^ (place // CAP * 2 + core)
        wanted = (target // splits) * SLOTS + place % CAP
        at = wanted[:, None, None] == placed_at.reshape(1, tok_rows, TOPK)
        return split_float(jnp.sum(jnp.where(at, late_weights[None], 0.0), axis=2), 2)

    place_weights = [weights_at(core) for core in (0, 1)]

    def weighted(core_blocks):
        return sum(
            lax.dot_general(
                part[first : first + rows.shape[0]],
                rows,
                (((0,), (0,)), ((), ())),
                preferred_element_type=jnp.float32,
            )
            for parts, (first, rows) in zip(place_weights, core_blocks)
            for part in parts
        )

    out = block_sum(whole_of(0)).astype(jnp.bfloat16)
    returned = [out]
    if line:
        mirror, beside, over = hops[1]
        mirror, hidden[2], returned[0], late_down = tie(mirror, hidden[2], out, unit_down)
        passed = along(mirror, OUTWARD)
        beside, over, mirror = tie(beside, over, mirror)
        hops[1] = [mirror, beside, over + passed]
    whole = whole_of(1)
    count = len(groups[1]) * 2 * CAP
    out = block_sum(whole[:count]).astype(jnp.bfloat16)
    if line:
        out, *hops[2][:2] = tie(out, *hops[2][:2])
    for index, offset in enumerate(groups[1]):
        returned.append(row_xor(out[index * 2 * CAP : (index + 1) * 2 * CAP], 2 * offset))
    if line:
        rest = whole[count:].reshape(8, cols_axis, hidden_part)[:, :, : 4 * LOW_STRIDE]
        rest = jnp.sum(rest.astype(jnp.float32), axis=1)
        rest = jnp.sum(rest.reshape(8, 2, 2, LOW_STRIDE), axis=1)[:, :, :tok_rows]
        low_sum = jnp.concatenate([rest[:, 0], rest[:, 1]], axis=0)
    else:
        low_sum = col_sum(partial_low)
    low_rank = low_sum.astype(jnp.bfloat16)
    expanded = jnp.where(select[:, None, :], low_rank[None], 0).reshape(
        adapter_count * RANK, tok_rows
    )
    branch = lax.dot_general(
        expanded, up_rows, (((0,), (0,)), ((), ())), preferred_element_type=jnp.float32
    )
    near = jnp.stack(returned)
    near_others = row_xor(near[:, CAP:], 1)
    if line:
        mirror, beside, facing = hops[2]
        part = block_sum(in_line(hidden[2], mirror, beside, jnp.zeros_like(mirror)))
        facing_down = lax.dynamic_slice(
            late_down, ((col_at ^ 2) * hidden_part, 0), (hidden_part, width_part)
        )
        facing, near, branch, part, facing_down, place_weights = tie(
            facing, near, branch, part, facing_down, place_weights
        )
        out = part + jnp.dot(facing, facing_down, preferred_element_type=jnp.float32)
    else:
        out = block_sum(whole_of(2))
    out = out.astype(jnp.bfloat16)
    far = [row_xor(out[:CAP], 2 * chips - 2), row_xor(out[CAP:], 2 * chips - 1)]
    near, out = tie(near, out)
    near = [near[:, :CAP].reshape(-1, width_part), near_others.reshape(-1, width_part)]
    mixed = branch + weighted([(0, rows) for rows in near])
    mixed = mixed + weighted([((chips - 1) * CAP, rows) for rows in far])
    return mixed.astype(jnp.bfloat16)


def solution(mesh):
    in_specs = (
        P("row", "col"),
        P("col"),
        P(),
        P(),
        P("row", None),
        P("row", None),
        P("row", "col", None),
        P("row", "col", None),
        P("row", None, "col"),
        P("row", "col", None),
        P("row", None, "col"),
    )
    out_specs = P("row", "col")
    return jax.shard_map(body, mesh=mesh, in_specs=in_specs, out_specs=out_specs, check_vma=False)
```

```python
import jax
import jax.numpy as jnp
from jax import lax
from jax.sharding import PartitionSpec as P

D = 2048
EXPERTS = 8
TOPK = 2
RANK = 16
CAP = 60
GAIN_ROWS = 8
LOW_STRIDE = 256
SLOTS = 64


def contract_last(left, right):
    return lax.dot_general(
        left, right, (((1,), (1,)), ((), ())), preferred_element_type=jnp.float32
    )


def col_shift(value, by):
    size = lax.axis_size("col")
    return lax.ppermute(value, "col", [(i, (i + by) % size) for i in range(size)])


def row_xor(value, by):
    return lax.ppermute(value, "row", [(i, i ^ by) for i in range(lax.axis_size("row"))])


def along(value, pairs):
    return lax.ppermute(value, "col", pairs)


BESIDE = [(0, 1), (1, 0), (2, 3), (3, 2)]
MIRROR = [(0, 3), (1, 2), (2, 1), (3, 0)]
OVER = [(0, 2), (3, 1)]
FACING = [(0, 2), (1, 3), (2, 0), (3, 1)]
OUTWARD = [(1, 0), (2, 3)]
ACROSS = [(1, 2), (2, 1)]


def first_hops(value, mirror, facing):
    return along(value, mirror), along(value, BESIDE), along(value, facing)


def in_line(value, mirror, beside, facing):
    here = lax.axis_index("col")
    return side_by_side(
        value, [(here ^ 1, 0, beside), (here ^ 3, 0, mirror), (here ^ 2, 0, facing)]
    )


def ring_gather(value):
    size = lax.axis_size("col")
    here = lax.axis_index("col")
    rows = value.shape[0]
    half = -(-rows // 16) * 8
    found = []
    from_left, from_right = value, value
    for hop in range(1, (size + 1) // 2):
        from_left, from_right = col_shift(from_left, 1), col_shift(from_right, -1)
        found += [
            (lax.rem(here + size - hop, size), 0, from_left),
            (lax.rem(here + hop, size), 0, from_right),
        ]
    if size % 2 == 0:
        facing = lax.rem(here + size // 2, size)
        found += [
            (facing, 0, col_shift(from_left[:half], 1)),
            (facing, half, col_shift(from_right[half:], -1)),
        ]
    return found


def side_by_side(value, others):
    rows, width = value.shape
    whole = jnp.zeros((rows, lax.axis_size("col") * width), value.dtype)
    for sender, first, block in [(lax.axis_index("col"), 0, value)] + others:
        whole = lax.dynamic_update_slice(whole, block, (first, sender * width))
    return whole


def col_sum(value):
    size = lax.axis_size("col")
    total = value
    for by in range(1, size):
        total = total + lax.ppermute(value, "col", [(i, i ^ by) for i in range(size)])
    return total


def both_cores(stacked):
    both = jnp.stack([stacked, row_xor(stacked, 1)], axis=1)
    return both.reshape((lax.axis_size("row"),) + stacked.shape[1:])


def normalised(features, rows):
    widened = features[:rows].astype(jnp.float32)
    gain = jnp.sum(features[rows : rows + 3].astype(jnp.float32), axis=0)
    scale = lax.rsqrt(jnp.mean(widened * widened, axis=1, keepdims=True) + 1e-06)
    return (widened * scale * gain[None, :]).astype(jnp.bfloat16)


def tie(*values):
    return lax.optimization_barrier(values)


def split_float(value, parts):
    pieces = []
    for _ in range(parts):
        piece = lax.reduce_precision(value, 8, 7)
        pieces.append(piece.astype(jnp.bfloat16))
        value = value - piece
    return pieces


def body(
    tokens,
    norm_gain,
    lengths,
    request_adapter,
    routes,
    route_weights,
    gate_weight,
    up_weight,
    down_weight,
    adapter_down,
    adapter_up,
):
    tok_rows, width_part = tokens.shape
    rows_axis, cols_axis = lax.axis_size("row"), lax.axis_size("col")
    row_at, col_at = lax.axis_index("row"), lax.axis_index("col")
    splits = rows_axis // EXPERTS
    chips = rows_axis // 2
    unit_gate, unit_up, unit_down = gate_weight[0], up_weight[0], down_weight[0]
    hidden_part = unit_gate.shape[0]
    line = cols_axis == 4

    gain_parts = jnp.stack(split_float(norm_gain, 3))
    sent = jnp.concatenate(
        [tokens, jnp.pad(gain_parts, ((0, GAIN_ROWS - 3), (0, 0)))], axis=0
    )
    hops = first_hops(sent, MIRROR, FACING) if line else ring_gather(sent)

    local_adapters = adapter_down.shape[0]
    mine = jnp.concatenate([jnp.transpose(adapter_down, (0, 2, 1)), adapter_up], axis=0)
    mine = mine.reshape(2 * local_adapters * RANK, width_part)
    by_chip = [mine] + [row_xor(mine, by) for by in range(2, rows_axis, 2)]
    assigned = routes.reshape(-1)
    assign_count = assigned.shape[0]
    expert_hot = (assigned[:, None] == jnp.arange(EXPERTS, dtype=jnp.int32)[None, :]).astype(
        jnp.bfloat16
    )
    earlier = (
        jnp.arange(assign_count, dtype=jnp.int32)[:, None]
        > jnp.arange(assign_count, dtype=jnp.int32)[None, :]
    ).astype(jnp.bfloat16)
    before = jnp.dot(earlier, expert_hot, preferred_element_type=jnp.float32)
    slot_index = jnp.sum(before * expert_hot.astype(jnp.float32), axis=1).astype(jnp.int32)
    placed_at = assigned * SLOTS + slot_index

    def placing(core, slots):
        place = jnp.arange(chips * slots, dtype=jnp.int32)
        target = row_at ^ (place // slots * 2 + core)
        wanted = (target // splits) * SLOTS + place % slots
        return (wanted[:, None] == placed_at[None, :]).astype(jnp.bfloat16)

    of_token = [
        jnp.sum(placing(core, SLOTS).reshape(-1, tok_rows, TOPK), axis=2) for core in (0, 1)
    ]
    if line:
        hops, of_token = tie(hops, of_token)
    features = in_line(sent, *hops) if line else side_by_side(sent, hops)
    normed, *by_chip = tie(normalised(features, tok_rows), *by_chip)

    def outgoing(core):
        placed = jnp.dot(of_token[core], normed, preferred_element_type=jnp.float32)
        return placed.astype(jnp.bfloat16).reshape(chips, SLOTS, D)

    there_half = outgoing(1)
    partner_own = row_xor(there_half[0], 1)
    partner_half = [partner_own] + list(row_xor(there_half[1:], 1))
    here_half = outgoing(0)

    groups = [[0], list(range(1, chips - 1)), [chips - 1]]
    pairs = [
        jnp.concatenate([here_half[offset], partner_half[offset]], axis=0)
        for offset in range(chips)
    ]
    for offset in range(1, chips):
        if offset == chips - 1:
            pairs[1:] = tie(*pairs[1:])
        pairs[offset] = row_xor(pairs[offset], 2 * offset)

    def hidden_of(offsets, earlier):
        arrived = jnp.concatenate(
            [
                pairs[offset][first : first + CAP]
                for offset in offsets
                for first in (0, SLOTS)
            ],
            axis=0,
        )
        arrived, *earlier = tie(arrived, *earlier)
        gate_sum = contract_last(arrived, unit_gate)
        up_sum = contract_last(arrived, unit_up)
        value = (jax.nn.silu(gate_sum) * up_sum).astype(jnp.bfloat16)
        return value, earlier

    def first_of(value, *pairs_of):
        return list(first_hops(value, *pairs_of)) if line else ring_gather(value)

    value, _ = hidden_of(groups[0], [])
    hidden, hops = [value], [first_of(value, MIRROR, OVER)]

    hidden[0], pairs[1:-1], by_chip = tie(hidden[0], pairs[1:-1], by_chip)
    factors = both_cores(jnp.stack(by_chip))
    factors = factors.reshape(rows_axis, 2, local_adapters * RANK, width_part)
    down_rows = factors[:, 0].reshape(-1, width_part)
    up_rows = factors[:, 1].reshape(-1, width_part)
    normed, pairs[1:-1] = tie(normed, pairs[1:-1])
    own = lax.dynamic_slice(normed, (0, col_at * width_part), (tok_rows, width_part))
    req_ends = jnp.cumsum(lengths)
    position = row_at * tok_rows + jnp.arange(tok_rows, dtype=jnp.int32)
    request = jnp.sum((position[None, :] >= req_ends[:, None]).astype(jnp.int32), axis=0)
    request_hot = request[None, :] == jnp.arange(lengths.shape[0], dtype=jnp.int32)[:, None]
    adapter = jnp.sum(jnp.where(request_hot, request_adapter[:, None], 0), axis=0)
    adapter_count = local_adapters * rows_axis
    order = jnp.arange(adapter_count, dtype=jnp.int32)
    held = (row_at ^ (order // local_adapters)) * local_adapters + order % local_adapters
    select = held[:, None] == adapter[None, :]
    projected = contract_last(down_rows, own).reshape(adapter_count, RANK, tok_rows)
    partial_low = jnp.sum(jnp.where(select[:, None, :], projected, 0.0), axis=0)
    extra = jnp.zeros((0, hidden_part), jnp.bfloat16)
    if line:
        pieces = [piece[at : at + 8] for piece in split_float(partial_low, 2) for at in (0, 8)]
        spare = (0, LOW_STRIDE - tok_rows)
        extra = jnp.concatenate([jnp.pad(piece, ((0, 0), spare)) for piece in pieces], axis=1)
        extra = jnp.pad(extra, ((0, 0), (0, hidden_part - extra.shape[1])))

    if line:
        hops[0][0], extra = tie(hops[0][0], extra)
    passed = along(hops[0][0], OUTWARD) if line else None
    value, (extra, *hops[0][:1]) = hidden_of(groups[1], [extra] + hops[0][:1])
    hidden.append(jnp.concatenate([value, extra], axis=0))
    hops.append(first_of(hidden[1], ACROSS, OVER))
    earlier = hops[0][1:] + [passed] if line else []
    pairs[-1], hidden[1] = tie(pairs[-1], hidden[1])
    value, (hidden[1], *earlier) = hidden_of(groups[2], [hidden[1]] + earlier)
    hidden.append(value)
    hops.append(first_of(value, MIRROR, OVER))
    if line:
        beside, over, passed = earlier
        hops[0] = [hops[0][0], beside, over + passed]

    def whole_of(number):
        return (in_line if line else side_by_side)(
            hidden[number], *(hops[number] if line else [hops[number]])
        )

    def block_sum(whole):
        return jnp.dot(whole, unit_down, preferred_element_type=jnp.float32)

    late_weights, hidden[2] = tie(route_weights, hidden[2])

    def weights_at(core):
        place = jnp.arange(chips * CAP, dtype=jnp.int32)
        target = row_at ^ (place // CAP * 2 + core)
        wanted = (target // splits) * SLOTS + place % CAP
        at = wanted[:, None, None] == placed_at.reshape(1, tok_rows, TOPK)
        return split_float(jnp.sum(jnp.where(at, late_weights[None], 0.0), axis=2), 2)

    place_weights = [weights_at(core) for core in (0, 1)]

    def weighted(core_blocks):
        return sum(
            lax.dot_general(
                part[first : first + rows.shape[0]],
                rows,
                (((0,), (0,)), ((), ())),
                preferred_element_type=jnp.float32,
            )
            for parts, (first, rows) in zip(place_weights, core_blocks)
            for part in parts
        )

    out = block_sum(whole_of(0)).astype(jnp.bfloat16)
    returned = [out]
    if line:
        mirror, beside, over = hops[1]
        mirror, hidden[2], returned[0], late_down = tie(mirror, hidden[2], out, unit_down)
        near = along(mirror, OUTWARD)
        beside, mirror = tie(beside, mirror)
        over, beside = tie(over, beside)
        hops[1] = [mirror + along(over, OUTWARD), beside, over + near]
        hops[2][0], over = tie(hops[2][0], over)
        hops[1][2] = over + near
        passed = along(hops[2][0], OUTWARD)
    whole = whole_of(1)
    count = len(groups[1]) * 2 * CAP
    out = block_sum(whole[:count]).astype(jnp.bfloat16)
    for index, offset in enumerate(groups[1]):
        returned.append(row_xor(out[index * 2 * CAP : (index + 1) * 2 * CAP], 2 * offset))
    if line:
        rest = whole[count:].reshape(8, cols_axis, hidden_part)[:, :, : 4 * LOW_STRIDE]
        rest = jnp.sum(rest.astype(jnp.float32), axis=1)
        rest = jnp.sum(rest.reshape(8, 2, 2, LOW_STRIDE), axis=1)[:, :, :tok_rows]
        low_sum = jnp.concatenate([rest[:, 0], rest[:, 1]], axis=0)
    else:
        low_sum = col_sum(partial_low)
    low_rank = low_sum.astype(jnp.bfloat16)
    expanded = jnp.where(select[:, None, :], low_rank[None], 0).reshape(
        adapter_count * RANK, tok_rows
    )
    branch = lax.dot_general(
        expanded, up_rows, (((0,), (0,)), ((), ())), preferred_element_type=jnp.float32
    )
    if line:
        mirror, beside, facing = hops[2]
        part = block_sum(in_line(hidden[2], mirror, beside, jnp.zeros_like(mirror)))
        facing_down = lax.dynamic_slice(
            late_down, ((col_at ^ 2) * hidden_part, 0), (hidden_part, width_part)
        )
        facing, passed, branch, part, facing_down, place_weights = tie(
            facing, passed, branch, part, facing_down, place_weights
        )
        out = part + jnp.dot(facing + passed, facing_down, preferred_element_type=jnp.float32)
    else:
        out = block_sum(whole_of(2))
    out = out.astype(jnp.bfloat16)
    returned.append(row_xor(out, 2 * chips - 2))
    near = jnp.stack(returned)
    near_others = row_xor(near[:, CAP:], 1)
    near = [near[:, :CAP].reshape(-1, width_part), near_others.reshape(-1, width_part)]
    mixed = branch + weighted([(0, rows) for rows in near])
    return mixed.astype(jnp.bfloat16)


def solution(mesh):
    in_specs = (
        P("row", "col"),
        P("col"),
        P(),
        P(),
        P("row", None),
        P("row", None),
        P("row", "col", None),
        P("row", "col", None),
        P("row", None, "col"),
        P("row", "col", None),
        P("row", None, "col"),
    )
    out_specs = P("row", "col")
    return jax.shard_map(body, mesh=mesh, in_specs=in_specs, out_specs=out_specs, check_vma=False)
```

```python
import jax
import jax.numpy as jnp
from jax import lax
from jax.experimental import pallas as pl
from jax.experimental.pallas import tpu as pltpu
from jax.sharding import PartitionSpec as P

D = 2048
EXPERTS = 8
TOPK = 2
RANK = 16
CAP = 60
GAIN_ROWS = 8
LOW_STRIDE = 256
SLOTS = 64


def contract_last(left, right):
    return lax.dot_general(
        left, right, (((1,), (1,)), ((), ())), preferred_element_type=jnp.float32
    )


def col_shift(value, by):
    size = lax.axis_size("col")
    return lax.ppermute(value, "col", [(i, (i + by) % size) for i in range(size)])


def row_xor(value, by):
    return lax.ppermute(value, "row", [(i, i ^ by) for i in range(lax.axis_size("row"))])


def along(value, pairs):
    return lax.ppermute(value, "col", pairs)


BESIDE = [(0, 1), (1, 0), (2, 3), (3, 2)]
MIRROR = [(0, 3), (1, 2), (2, 1), (3, 0)]
OVER = [(0, 2), (3, 1)]
FACING = [(0, 2), (1, 3), (2, 0), (3, 1)]
OUTWARD = [(1, 0), (2, 3)]
ACROSS = [(1, 2), (2, 1)]


def first_hops(value, mirror, facing):
    return along(value, mirror), along(value, BESIDE), along(value, facing)


def in_line(value, mirror, beside, facing):
    here = lax.axis_index("col")
    return side_by_side(
        value, [(here ^ 1, 0, beside), (here ^ 3, 0, mirror), (here ^ 2, 0, facing)]
    )


def ring_gather(value):
    size = lax.axis_size("col")
    here = lax.axis_index("col")
    rows = value.shape[0]
    half = -(-rows // 16) * 8
    found = []
    from_left, from_right = value, value
    for hop in range(1, (size + 1) // 2):
        from_left, from_right = col_shift(from_left, 1), col_shift(from_right, -1)
        found += [
            (lax.rem(here + size - hop, size), 0, from_left),
            (lax.rem(here + hop, size), 0, from_right),
        ]
    if size % 2 == 0:
        facing = lax.rem(here + size // 2, size)
        found += [
            (facing, 0, col_shift(from_left[:half], 1)),
            (facing, half, col_shift(from_right[half:], -1)),
        ]
    return found


def side_by_side(value, others):
    rows, width = value.shape
    whole = jnp.zeros((rows, lax.axis_size("col") * width), value.dtype)
    for sender, first, block in [(lax.axis_index("col"), 0, value)] + others:
        whole = lax.dynamic_update_slice(whole, block, (first, sender * width))
    return whole


def col_sum(value):
    size = lax.axis_size("col")
    total = value
    for by in range(1, size):
        total = total + lax.ppermute(value, "col", [(i, i ^ by) for i in range(size)])
    return total


def both_cores(stacked):
    both = jnp.stack([stacked, row_xor(stacked, 1)], axis=1)
    return both.reshape((lax.axis_size("row"),) + stacked.shape[1:])


def normalised(features, rows):
    widened = features[:rows].astype(jnp.float32)
    gain = jnp.sum(features[rows : rows + 3].astype(jnp.float32), axis=0)
    scale = lax.rsqrt(jnp.mean(widened * widened, axis=1, keepdims=True) + 1e-06)
    return (widened * scale * gain[None, :]).astype(jnp.bfloat16)


def line_normalised(value, mirror, beside, facing, rows):
    width = value.shape[1]

    def kernel(at_ref, *refs):
        *block_refs, out_ref = refs
        at = at_ref[0]
        blocks = [ref[...].astype(jnp.float32) for ref in block_refs]
        squares = sum(jnp.sum(block[:rows] * block[:rows], axis=1, keepdims=True) for block in blocks)
        scale = lax.rsqrt(squares / (4 * width) + 1e-06)
        for block, away in zip(blocks, (0, 3, 1, 2)):
            gain = jnp.sum(block[rows:], axis=0, keepdims=True)
            where = pl.ds(pl.multiple_of((at ^ away) * width, width), width)
            out_ref[:, where] = (block[:rows] * scale * gain).astype(out_ref.dtype)

    return pl.pallas_call(
        kernel,
        out_shape=jax.ShapeDtypeStruct((rows, 4 * width), jnp.bfloat16),
        in_specs=[pl.BlockSpec(memory_space=pltpu.SMEM)]
        + [pl.BlockSpec(memory_space=pltpu.VMEM)] * 4,
        out_specs=pl.BlockSpec(memory_space=pltpu.VMEM),
        compiler_params=pltpu.CompilerParams(vmem_limit_bytes=16 * 1024 * 1024),
        cost_estimate=pl.CostEstimate(
            flops=16 * rows * width, bytes_accessed=16 * rows * width, transcendentals=rows
        ),
    )(lax.axis_index("col")[None], value, mirror, beside, facing)


def tie(*values):
    return lax.optimization_barrier(values)


def split_float(value, parts):
    pieces = []
    for _ in range(parts):
        piece = lax.reduce_precision(value, 8, 7)
        pieces.append(piece.astype(jnp.bfloat16))
        value = value - piece
    return pieces


def body(
    tokens,
    norm_gain,
    lengths,
    request_adapter,
    routes,
    route_weights,
    gate_weight,
    up_weight,
    down_weight,
    adapter_down,
    adapter_up,
):
    tok_rows, width_part = tokens.shape
    rows_axis, cols_axis = lax.axis_size("row"), lax.axis_size("col")
    row_at, col_at = lax.axis_index("row"), lax.axis_index("col")
    splits = rows_axis // EXPERTS
    chips = rows_axis // 2
    unit_gate, unit_up, unit_down = gate_weight[0], up_weight[0], down_weight[0]
    hidden_part = unit_gate.shape[0]
    line = cols_axis == 4

    gain_parts = jnp.stack(split_float(norm_gain, 3))
    sent = jnp.concatenate(
        [tokens, jnp.pad(gain_parts, ((0, GAIN_ROWS - 3), (0, 0)))], axis=0
    )
    hops = list(first_hops(sent, MIRROR, FACING)) if line else ring_gather(sent)

    local_adapters = adapter_down.shape[0]
    mine = jnp.concatenate([jnp.transpose(adapter_down, (0, 2, 1)), adapter_up], axis=0)
    mine = mine.reshape(2 * local_adapters * RANK, width_part)
    by_chip = [mine] + [row_xor(mine, by) for by in range(2, rows_axis - 2, 2)]
    if line:
        hops[0], mine = tie(hops[0], mine)
    by_chip.append(row_xor(mine, rows_axis - 2))
    assigned = routes.reshape(-1)
    assign_count = assigned.shape[0]
    expert_hot = (assigned[:, None] == jnp.arange(EXPERTS, dtype=jnp.int32)[None, :]).astype(
        jnp.bfloat16
    )
    earlier = (
        jnp.arange(assign_count, dtype=jnp.int32)[:, None]
        > jnp.arange(assign_count, dtype=jnp.int32)[None, :]
    ).astype(jnp.bfloat16)
    before = jnp.dot(earlier, expert_hot, preferred_element_type=jnp.float32)
    slot_index = jnp.sum(before * expert_hot.astype(jnp.float32), axis=1).astype(jnp.int32)
    placed_at = assigned * SLOTS + slot_index

    def placing(core, slots):
        place = jnp.arange(chips * slots, dtype=jnp.int32)
        target = row_at ^ (place // slots * 2 + core)
        wanted = (target // splits) * SLOTS + place % slots
        return (wanted[:, None] == placed_at[None, :]).astype(jnp.bfloat16)

    of_token = [
        jnp.sum(placing(core, SLOTS).reshape(-1, tok_rows, TOPK), axis=2) for core in (0, 1)
    ]
    if line:
        hops, of_token = tie(hops, of_token)
    if line:
        normed = line_normalised(sent, *hops, tok_rows)
    else:
        normed = normalised(side_by_side(sent, hops), tok_rows)
    normed, *by_chip[:-1] = tie(normed, *by_chip[:-1])

    def outgoing(core):
        placed = jnp.dot(of_token[core], normed, preferred_element_type=jnp.float32)
        return placed.astype(jnp.bfloat16).reshape(chips, SLOTS, D)

    there_half = outgoing(1)
    partner_own = row_xor(there_half[0], 1)
    partner_half = [partner_own] + list(row_xor(there_half[1:], 1))
    here_half = outgoing(0)

    groups = [[0], list(range(1, chips - 1)), [chips - 1]]
    pairs = [
        jnp.concatenate([here_half[offset], partner_half[offset]], axis=0)
        for offset in range(chips)
    ]
    if line:
        pairs[1], by_chip[-1] = tie(pairs[1], by_chip[-1])
    for offset in range(1, chips):
        if offset == chips - 1:
            pairs[1:] = tie(*pairs[1:])
        pairs[offset] = row_xor(pairs[offset], 2 * offset)

    def hidden_of(offsets, earlier):
        arrived = jnp.concatenate(
            [
                pairs[offset][first : first + CAP]
                for offset in offsets
                for first in (0, SLOTS)
            ],
            axis=0,
        )
        arrived, *earlier = tie(arrived, *earlier)
        gate_sum = contract_last(arrived, unit_gate)
        up_sum = contract_last(arrived, unit_up)
        value = (jax.nn.silu(gate_sum) * up_sum).astype(jnp.bfloat16)
        return value, earlier

    def first_of(value, *pairs_of):
        return list(first_hops(value, *pairs_of)) if line else ring_gather(value)

    value, _ = hidden_of(groups[0], [])
    hidden, hops = [value], [first_of(value, MIRROR, OVER)]

    hidden[0], pairs[1:-1], by_chip = tie(hidden[0], pairs[1:-1], by_chip)
    factors = both_cores(jnp.stack(by_chip))
    factors = factors.reshape(rows_axis, 2, local_adapters * RANK, width_part)
    down_rows = factors[:, 0].reshape(-1, width_part)
    up_rows = factors[:, 1].reshape(-1, width_part)
    normed, pairs[1:-1] = tie(normed, pairs[1:-1])
    own = lax.dynamic_slice(normed, (0, col_at * width_part), (tok_rows, width_part))
    req_ends = jnp.cumsum(lengths)
    position = row_at * tok_rows + jnp.arange(tok_rows, dtype=jnp.int32)
    request = jnp.sum((position[None, :] >= req_ends[:, None]).astype(jnp.int32), axis=0)
    request_hot = request[None, :] == jnp.arange(lengths.shape[0], dtype=jnp.int32)[:, None]
    adapter = jnp.sum(jnp.where(request_hot, request_adapter[:, None], 0), axis=0)
    adapter_count = local_adapters * rows_axis
    order = jnp.arange(adapter_count, dtype=jnp.int32)
    held = (row_at ^ (order // local_adapters)) * local_adapters + order % local_adapters
    select = held[:, None] == adapter[None, :]
    projected = contract_last(down_rows, own).reshape(adapter_count, RANK, tok_rows)
    partial_low = jnp.sum(jnp.where(select[:, None, :], projected, 0.0), axis=0)
    extra = jnp.zeros((0, hidden_part), jnp.bfloat16)
    if line:
        pieces = [piece[at : at + 8] for piece in split_float(partial_low, 2) for at in (0, 8)]
        spare = (0, LOW_STRIDE - tok_rows)
        extra = jnp.concatenate([jnp.pad(piece, ((0, 0), spare)) for piece in pieces], axis=1)
        extra = jnp.pad(extra, ((0, 0), (0, hidden_part - extra.shape[1])))

    if line:
        hops[0][0], extra = tie(hops[0][0], extra)
    passed = along(hops[0][0], OUTWARD) if line else None
    value, (extra, *hops[0][:2]) = hidden_of(groups[1], [extra] + hops[0][:2])
    hidden.append(jnp.concatenate([value, extra], axis=0))
    hops.append(first_of(hidden[1], ACROSS, OVER))
    earlier = hops[0][1:] + [passed] if line else []
    pairs[-1], hidden[1] = tie(pairs[-1], hidden[1])
    value, (hidden[1], *earlier) = hidden_of(groups[2], [hidden[1]] + earlier)
    hidden.append(value)
    hops.append(first_of(value, MIRROR, OVER))
    if line:
        beside, over, passed = earlier
        hops[0] = [hops[0][0], beside, over + passed]

    def whole_of(number):
        return (in_line if line else side_by_side)(
            hidden[number], *(hops[number] if line else [hops[number]])
        )

    def block_sum(whole):
        return jnp.dot(whole, unit_down, preferred_element_type=jnp.float32)

    late_weights, hidden[2] = tie(route_weights, hidden[2])

    def weights_at(core):
        place = jnp.arange(chips * CAP, dtype=jnp.int32)
        target = row_at ^ (place // CAP * 2 + core)
        wanted = (target // splits) * SLOTS + place % CAP
        at = wanted[:, None, None] == placed_at.reshape(1, tok_rows, TOPK)
        return split_float(jnp.sum(jnp.where(at, late_weights[None], 0.0), axis=2), 2)

    place_weights = [weights_at(core) for core in (0, 1)]

    def weighted(core_blocks):
        return sum(
            lax.dot_general(
                part[first : first + rows.shape[0]],
                rows,
                (((0,), (0,)), ((), ())),
                preferred_element_type=jnp.float32,
            )
            for parts, (first, rows) in zip(place_weights, core_blocks)
            for part in parts
        )

    out = block_sum(whole_of(0)).astype(jnp.bfloat16)
    returned = [out]
    if line:
        mirror, beside, over = hops[1]
        mirror, hidden[2], returned[0], late_down = tie(mirror, hidden[2], out, unit_down)
        near = along(mirror, OUTWARD)
        beside, mirror = tie(beside, mirror)
        over, beside = tie(over, beside)
        hops[1] = [mirror + along(over, OUTWARD), beside, over + near]
        hops[2][0], over = tie(hops[2][0], over)
        hops[1][2] = over + near
        passed = along(hops[2][0], OUTWARD)
    whole = whole_of(1)
    count = len(groups[1]) * 2 * CAP
    out = block_sum(whole[:count]).astype(jnp.bfloat16)
    for index, offset in enumerate(groups[1]):
        returned.append(row_xor(out[index * 2 * CAP : (index + 1) * 2 * CAP], 2 * offset))
    if line:
        rest = whole[count:].reshape(8, cols_axis, hidden_part)[:, :, : 4 * LOW_STRIDE]
        rest = jnp.sum(rest.astype(jnp.float32), axis=1)
        rest = jnp.sum(rest.reshape(8, 2, 2, LOW_STRIDE), axis=1)[:, :, :tok_rows]
        low_sum = jnp.concatenate([rest[:, 0], rest[:, 1]], axis=0)
    else:
        low_sum = col_sum(partial_low)
    low_rank = low_sum.astype(jnp.bfloat16)
    expanded = jnp.where(select[:, None, :], low_rank[None], 0).reshape(
        adapter_count * RANK, tok_rows
    )
    branch = lax.dot_general(
        expanded, up_rows, (((0,), (0,)), ((), ())), preferred_element_type=jnp.float32
    )
    if line:
        mirror, beside, facing = hops[2]
        part = block_sum(in_line(hidden[2], mirror, beside, jnp.zeros_like(mirror)))
        facing_down = lax.dynamic_slice(
            late_down, ((col_at ^ 2) * hidden_part, 0), (hidden_part, width_part)
        )
        facing, passed, branch, part, facing_down, place_weights = tie(
            facing, passed, branch, part, facing_down, place_weights
        )
        out = part + jnp.dot(facing + passed, facing_down, preferred_element_type=jnp.float32)
    else:
        out = block_sum(whole_of(2))
    out = out.astype(jnp.bfloat16)
    returned.append(row_xor(out, 2 * chips - 2))
    near = jnp.stack(returned)
    near_others = row_xor(near[:, CAP:], 1)
    near = [near[:, :CAP].reshape(-1, width_part), near_others.reshape(-1, width_part)]
    mixed = branch + weighted([(0, rows) for rows in near])
    return mixed.astype(jnp.bfloat16)


def solution(mesh):
    in_specs = (
        P("row", "col"),
        P("col"),
        P(),
        P(),
        P("row", None),
        P("row", None),
        P("row", "col", None),
        P("row", "col", None),
        P("row", None, "col"),
        P("row", "col", None),
        P("row", None, "col"),
    )
    out_specs = P("row", "col")
    return jax.shard_map(body, mesh=mesh, in_specs=in_specs, out_specs=out_specs, check_vma=False)
```

```python
import jax
import jax.numpy as jnp
from jax import lax
from jax.experimental import pallas as pl
from jax.experimental.pallas import tpu as pltpu
from jax.sharding import PartitionSpec as P

D = 2048
EXPERTS = 8
TOPK = 2
RANK = 16
CAP = 60
GAIN_ROWS = 8
LOW_STRIDE = 256
SLOTS = 64


def contract_last(left, right):
    return lax.dot_general(
        left, right, (((1,), (1,)), ((), ())), preferred_element_type=jnp.float32
    )


def col_shift(value, by):
    size = lax.axis_size("col")
    return lax.ppermute(value, "col", [(i, (i + by) % size) for i in range(size)])


def row_xor(value, by):
    return lax.ppermute(value, "row", [(i, i ^ by) for i in range(lax.axis_size("row"))])


def along(value, pairs):
    return lax.ppermute(value, "col", pairs)


BESIDE = [(0, 1), (1, 0), (2, 3), (3, 2)]
MIRROR = [(0, 3), (1, 2), (2, 1), (3, 0)]
OVER = [(0, 2), (3, 1)]
FACING = [(0, 2), (1, 3), (2, 0), (3, 1)]
OUTWARD = [(1, 0), (2, 3)]
ACROSS = [(1, 2), (2, 1)]


def first_hops(value, mirror, facing):
    return along(value, mirror), along(value, BESIDE), along(value, facing)


def in_line(value, mirror, beside, facing):
    here = lax.axis_index("col")
    return side_by_side(
        value, [(here ^ 1, 0, beside), (here ^ 3, 0, mirror), (here ^ 2, 0, facing)]
    )


def ring_gather(value):
    size = lax.axis_size("col")
    here = lax.axis_index("col")
    rows = value.shape[0]
    half = -(-rows // 16) * 8
    found = []
    from_left, from_right = value, value
    for hop in range(1, (size + 1) // 2):
        from_left, from_right = col_shift(from_left, 1), col_shift(from_right, -1)
        found += [
            (lax.rem(here + size - hop, size), 0, from_left),
            (lax.rem(here + hop, size), 0, from_right),
        ]
    if size % 2 == 0:
        facing = lax.rem(here + size // 2, size)
        found += [
            (facing, 0, col_shift(from_left[:half], 1)),
            (facing, half, col_shift(from_right[half:], -1)),
        ]
    return found


def side_by_side(value, others):
    rows, width = value.shape
    whole = jnp.zeros((rows, lax.axis_size("col") * width), value.dtype)
    for sender, first, block in [(lax.axis_index("col"), 0, value)] + others:
        whole = lax.dynamic_update_slice(whole, block, (first, sender * width))
    return whole


def col_sum(value):
    size = lax.axis_size("col")
    total = value
    for by in range(1, size):
        total = total + lax.ppermute(value, "col", [(i, i ^ by) for i in range(size)])
    return total


def both_cores(stacked):
    both = jnp.stack([stacked, row_xor(stacked, 1)], axis=1)
    return both.reshape((lax.axis_size("row"),) + stacked.shape[1:])


def normalised(features, rows):
    widened = features[:rows].astype(jnp.float32)
    gain = jnp.sum(features[rows : rows + 3].astype(jnp.float32), axis=0)
    scale = lax.rsqrt(jnp.mean(widened * widened, axis=1, keepdims=True) + 1e-06)
    return (widened * scale * gain[None, :]).astype(jnp.bfloat16)


def line_normalised(value, mirror, beside, facing, rows):
    width = value.shape[1]

    def kernel(at_ref, *refs):
        *block_refs, out_ref = refs
        at = at_ref[0]
        blocks = [ref[...].astype(jnp.float32) for ref in block_refs]
        squares = sum(jnp.sum(block[:rows] * block[:rows], axis=1, keepdims=True) for block in blocks)
        scale = lax.rsqrt(squares / (4 * width) + 1e-06)
        for block, away in zip(blocks, (0, 3, 1, 2)):
            gain = jnp.sum(block[rows:], axis=0, keepdims=True)
            where = pl.ds(pl.multiple_of((at ^ away) * width, width), width)
            out_ref[:, where] = (block[:rows] * scale * gain).astype(out_ref.dtype)

    return pl.pallas_call(
        kernel,
        out_shape=jax.ShapeDtypeStruct((rows, 4 * width), jnp.bfloat16),
        in_specs=[pl.BlockSpec(memory_space=pltpu.SMEM)]
        + [pl.BlockSpec(memory_space=pltpu.VMEM)] * 4,
        out_specs=pl.BlockSpec(memory_space=pltpu.VMEM),
        compiler_params=pltpu.CompilerParams(vmem_limit_bytes=16 * 1024 * 1024),
        cost_estimate=pl.CostEstimate(
            flops=16 * rows * width, bytes_accessed=16 * rows * width, transcendentals=rows
        ),
    )(lax.axis_index("col")[None], value, mirror, beside, facing)


def tie(*values):
    return lax.optimization_barrier(values)


def split_float(value, parts):
    pieces = []
    for _ in range(parts):
        piece = lax.reduce_precision(value, 8, 7)
        pieces.append(piece.astype(jnp.bfloat16))
        value = value - piece
    return pieces


def body(
    tokens,
    norm_gain,
    lengths,
    request_adapter,
    routes,
    route_weights,
    gate_weight,
    up_weight,
    down_weight,
    adapter_down,
    adapter_up,
):
    tok_rows, width_part = tokens.shape
    rows_axis, cols_axis = lax.axis_size("row"), lax.axis_size("col")
    row_at, col_at = lax.axis_index("row"), lax.axis_index("col")
    splits = rows_axis // EXPERTS
    chips = rows_axis // 2
    unit_gate, unit_up, unit_down = gate_weight[0], up_weight[0], down_weight[0]
    hidden_part = unit_gate.shape[0]
    line = cols_axis == 4

    gain_parts = jnp.stack(split_float(norm_gain, 3))
    sent = jnp.concatenate(
        [tokens, jnp.pad(gain_parts, ((0, GAIN_ROWS - 3), (0, 0)))], axis=0
    )
    hops = list(first_hops(sent, MIRROR, FACING)) if line else ring_gather(sent)

    local_adapters = adapter_down.shape[0]
    mine = jnp.concatenate([jnp.transpose(adapter_down, (0, 2, 1)), adapter_up], axis=0)
    mine = mine.reshape(2 * local_adapters * RANK, width_part)
    by_chip = [mine] + [row_xor(mine, by) for by in range(2, rows_axis - 2, 2)]
    if line:
        hops[0], mine = tie(hops[0], mine)
    by_chip.append(row_xor(mine, rows_axis - 2))
    assigned = routes.reshape(-1)
    assign_count = assigned.shape[0]
    expert_hot = (assigned[:, None] == jnp.arange(EXPERTS, dtype=jnp.int32)[None, :]).astype(
        jnp.bfloat16
    )
    earlier = (
        jnp.arange(assign_count, dtype=jnp.int32)[:, None]
        > jnp.arange(assign_count, dtype=jnp.int32)[None, :]
    ).astype(jnp.bfloat16)
    before = jnp.dot(earlier, expert_hot, preferred_element_type=jnp.float32)
    slot_index = jnp.sum(before * expert_hot.astype(jnp.float32), axis=1).astype(jnp.int32)
    placed_at = assigned * SLOTS + slot_index

    def placing(core, slots):
        place = jnp.arange(chips * slots, dtype=jnp.int32)
        target = row_at ^ (place // slots * 2 + core)
        wanted = (target // splits) * SLOTS + place % slots
        return (wanted[:, None] == placed_at[None, :]).astype(jnp.bfloat16)

    of_token = [
        jnp.sum(placing(core, SLOTS).reshape(-1, tok_rows, TOPK), axis=2) for core in (0, 1)
    ]
    if line:
        hops, of_token = tie(hops, of_token)
    if line:
        normed = line_normalised(sent, *hops, tok_rows)
    else:
        normed = normalised(side_by_side(sent, hops), tok_rows)
    normed, *by_chip[:-1] = tie(normed, *by_chip[:-1])

    def outgoing(core):
        placed = jnp.dot(of_token[core], normed, preferred_element_type=jnp.float32)
        return placed.astype(jnp.bfloat16).reshape(chips, SLOTS, D)

    there_half = outgoing(1)
    partner_own = row_xor(there_half[0], 1)
    partner_half = [partner_own] + list(row_xor(there_half[1:], 1))
    here_half = outgoing(0)

    groups = [[0], list(range(1, chips - 1)), [chips - 1]]
    pairs = [
        jnp.concatenate([here_half[offset], partner_half[offset]], axis=0)
        for offset in range(chips)
    ]
    if line:
        pairs[1], pairs[2], by_chip[-1] = tie(pairs[1], pairs[2], by_chip[-1])
    for offset in range(1, chips):
        if offset == chips - 1:
            pairs[1:] = tie(*pairs[1:])
        pairs[offset] = row_xor(pairs[offset], 2 * offset)

    def hidden_of(offsets, earlier):
        arrived = jnp.concatenate(
            [
                pairs[offset][first : first + CAP]
                for offset in offsets
                for first in (0, SLOTS)
            ],
            axis=0,
        )
        arrived, *earlier = tie(arrived, *earlier)
        gate_sum = contract_last(arrived, unit_gate)
        up_sum = contract_last(arrived, unit_up)
        value = (jax.nn.silu(gate_sum) * up_sum).astype(jnp.bfloat16)
        return value, earlier

    def first_of(value, *pairs_of):
        return list(first_hops(value, *pairs_of)) if line else ring_gather(value)

    value, _ = hidden_of(groups[0], [])
    hidden, hops = [value], [first_of(value, MIRROR, OVER)]

    hidden[0], pairs[1:-1], by_chip = tie(hidden[0], pairs[1:-1], by_chip)
    factors = both_cores(jnp.stack(by_chip))
    factors = factors.reshape(rows_axis, 2, local_adapters * RANK, width_part)
    down_rows = factors[:, 0].reshape(-1, width_part)
    up_rows = factors[:, 1].reshape(-1, width_part)
    normed, pairs[1:-1] = tie(normed, pairs[1:-1])
    own = lax.dynamic_slice(normed, (0, col_at * width_part), (tok_rows, width_part))
    req_ends = jnp.cumsum(lengths)
    position = row_at * tok_rows + jnp.arange(tok_rows, dtype=jnp.int32)
    request = jnp.sum((position[None, :] >= req_ends[:, None]).astype(jnp.int32), axis=0)
    request_hot = request[None, :] == jnp.arange(lengths.shape[0], dtype=jnp.int32)[:, None]
    adapter = jnp.sum(jnp.where(request_hot, request_adapter[:, None], 0), axis=0)
    adapter_count = local_adapters * rows_axis
    order = jnp.arange(adapter_count, dtype=jnp.int32)
    held = (row_at ^ (order // local_adapters)) * local_adapters + order % local_adapters
    select = held[:, None] == adapter[None, :]
    projected = contract_last(down_rows, own).reshape(adapter_count, RANK, tok_rows)
    partial_low = jnp.sum(jnp.where(select[:, None, :], projected, 0.0), axis=0)
    extra = jnp.zeros((0, hidden_part), jnp.bfloat16)
    if line:
        pieces = [piece[at : at + 8] for piece in split_float(partial_low, 2) for at in (0, 8)]
        spare = (0, LOW_STRIDE - tok_rows)
        extra = jnp.concatenate([jnp.pad(piece, ((0, 0), spare)) for piece in pieces], axis=1)
        extra = jnp.pad(extra, ((0, 0), (0, hidden_part - extra.shape[1])))

    if line:
        hops[0][0], extra = tie(hops[0][0], extra)
    passed = along(hops[0][0], OUTWARD) if line else None
    value, (extra, *hops[0][:2]) = hidden_of(groups[1], [extra] + hops[0][:2])
    hidden.append(jnp.concatenate([value, extra], axis=0))
    hops.append(first_of(hidden[1], ACROSS, OVER))
    earlier = hops[0][1:] + [passed] if line else []
    pairs[-1], hidden[1] = tie(pairs[-1], hidden[1])
    value, (hidden[1], *earlier) = hidden_of(groups[2], [hidden[1]] + earlier)
    hidden.append(value)
    hops.append(first_of(value, MIRROR, OVER))
    if line:
        beside, over, passed = earlier
        hops[0] = [hops[0][0], beside, over + passed]

    def whole_of(number):
        return (in_line if line else side_by_side)(
            hidden[number], *(hops[number] if line else [hops[number]])
        )

    def block_sum(whole):
        return jnp.dot(whole, unit_down, preferred_element_type=jnp.float32)

    late_weights, hidden[2] = tie(route_weights, hidden[2])

    def weights_at(core):
        place = jnp.arange(chips * CAP, dtype=jnp.int32)
        target = row_at ^ (place // CAP * 2 + core)
        wanted = (target // splits) * SLOTS + place % CAP
        at = wanted[:, None, None] == placed_at.reshape(1, tok_rows, TOPK)
        return split_float(jnp.sum(jnp.where(at, late_weights[None], 0.0), axis=2), 2)

    place_weights = [weights_at(core) for core in (0, 1)]

    def weighted(core_blocks):
        return sum(
            lax.dot_general(
                part[first : first + rows.shape[0]],
                rows,
                (((0,), (0,)), ((), ())),
                preferred_element_type=jnp.float32,
            )
            for parts, (first, rows) in zip(place_weights, core_blocks)
            for part in parts
        )

    out = block_sum(whole_of(0)).astype(jnp.bfloat16)
    returned = [out]
    if line:
        mirror, beside, over = hops[1]
        mirror, hidden[2], returned[0], late_down = tie(mirror, hidden[2], out, unit_down)
        near = along(mirror, OUTWARD)
        beside, mirror = tie(beside, mirror)
        over, beside = tie(over, beside)
        hops[1] = [mirror + along(over, OUTWARD), beside, over + near]
        hops[2][0], over = tie(hops[2][0], over)
        hops[1][2] = over + near
        passed = along(hops[2][0], OUTWARD)
    whole = whole_of(1)
    count = len(groups[1]) * 2 * CAP
    out = block_sum(whole[:count]).astype(jnp.bfloat16)
    for index, offset in enumerate(groups[1]):
        returned.append(row_xor(out[index * 2 * CAP : (index + 1) * 2 * CAP], 2 * offset))
    if line:
        rest = whole[count:].reshape(8, cols_axis, hidden_part)[:, :, : 4 * LOW_STRIDE]
        rest = jnp.sum(rest.astype(jnp.float32), axis=1)
        rest = jnp.sum(rest.reshape(8, 2, 2, LOW_STRIDE), axis=1)[:, :, :tok_rows]
        low_sum = jnp.concatenate([rest[:, 0], rest[:, 1]], axis=0)
    else:
        low_sum = col_sum(partial_low)
    low_rank = low_sum.astype(jnp.bfloat16)
    expanded = jnp.where(select[:, None, :], low_rank[None], 0).reshape(
        adapter_count * RANK, tok_rows
    )
    branch = lax.dot_general(
        expanded, up_rows, (((0,), (0,)), ((), ())), preferred_element_type=jnp.float32
    )
    if line:
        mirror, beside, facing = hops[2]
        part = block_sum(in_line(hidden[2], mirror, beside, jnp.zeros_like(mirror)))
        facing_down = lax.dynamic_slice(
            late_down, ((col_at ^ 2) * hidden_part, 0), (hidden_part, width_part)
        )
        facing, passed, branch, part, facing_down = tie(
            facing, passed, branch, part, facing_down
        )
        out = part + jnp.dot(facing + passed, facing_down, preferred_element_type=jnp.float32)
    else:
        out = block_sum(whole_of(2))
    out = out.astype(jnp.bfloat16)
    returned.append(row_xor(out, 2 * chips - 2))
    near = jnp.stack(returned)
    near_others = row_xor(near[:, CAP:], 1)
    near = [near[:, :CAP].reshape(-1, width_part), near_others.reshape(-1, width_part)]
    mixed = branch + weighted([(0, rows) for rows in near])
    return mixed.astype(jnp.bfloat16)


def solution(mesh):
    in_specs = (
        P("row", "col"),
        P("col"),
        P(),
        P(),
        P("row", None),
        P("row", None),
        P("row", "col", None),
        P("row", "col", None),
        P("row", None, "col"),
        P("row", "col", None),
        P("row", None, "col"),
    )
    out_specs = P("row", "col")
    return jax.shard_map(body, mesh=mesh, in_specs=in_specs, out_specs=out_specs, check_vma=False)
```

```python
import jax
import jax.numpy as jnp
from jax import lax
from jax.experimental import pallas as pl
from jax.experimental.pallas import tpu as pltpu
from jax.sharding import PartitionSpec as P

D = 2048
EXPERTS = 8
TOPK = 2
RANK = 16
CAP = 60
GAIN_ROWS = 8
LOW_STRIDE = 256
SLOTS = 64


def contract_last(left, right):
    return lax.dot_general(
        left, right, (((1,), (1,)), ((), ())), preferred_element_type=jnp.float32
    )


def col_shift(value, by):
    size = lax.axis_size("col")
    return lax.ppermute(value, "col", [(i, (i + by) % size) for i in range(size)])


def row_xor(value, by):
    return lax.ppermute(value, "row", [(i, i ^ by) for i in range(lax.axis_size("row"))])


def along(value, pairs):
    return lax.ppermute(value, "col", pairs)


BESIDE = [(0, 1), (1, 0), (2, 3), (3, 2)]
MIRROR = [(0, 3), (1, 2), (2, 1), (3, 0)]
OVER = [(0, 2), (3, 1)]
FACING = [(0, 2), (1, 3), (2, 0), (3, 1)]
OUTWARD = [(1, 0), (2, 3)]
ACROSS = [(1, 2), (2, 1)]


def first_hops(value, mirror, facing):
    return along(value, mirror), along(value, BESIDE), along(value, facing)


def in_line(value, mirror, beside, facing):
    here = lax.axis_index("col")
    return side_by_side(
        value, [(here ^ 1, 0, beside), (here ^ 3, 0, mirror), (here ^ 2, 0, facing)]
    )


def ring_gather(value):
    size = lax.axis_size("col")
    here = lax.axis_index("col")
    rows = value.shape[0]
    half = -(-rows // 16) * 8
    found = []
    from_left, from_right = value, value
    for hop in range(1, (size + 1) // 2):
        from_left, from_right = col_shift(from_left, 1), col_shift(from_right, -1)
        found += [
            (lax.rem(here + size - hop, size), 0, from_left),
            (lax.rem(here + hop, size), 0, from_right),
        ]
    if size % 2 == 0:
        facing = lax.rem(here + size // 2, size)
        found += [
            (facing, 0, col_shift(from_left[:half], 1)),
            (facing, half, col_shift(from_right[half:], -1)),
        ]
    return found


def side_by_side(value, others):
    rows, width = value.shape
    whole = jnp.zeros((rows, lax.axis_size("col") * width), value.dtype)
    for sender, first, block in [(lax.axis_index("col"), 0, value)] + others:
        whole = lax.dynamic_update_slice(whole, block, (first, sender * width))
    return whole


def col_sum(value):
    size = lax.axis_size("col")
    total = value
    for by in range(1, size):
        total = total + lax.ppermute(value, "col", [(i, i ^ by) for i in range(size)])
    return total


def both_cores(stacked):
    both = jnp.stack([stacked, row_xor(stacked, 1)], axis=1)
    return both.reshape((lax.axis_size("row"),) + stacked.shape[1:])


def normalised(features, rows):
    widened = features[:rows].astype(jnp.float32)
    gain = jnp.sum(features[rows : rows + 3].astype(jnp.float32), axis=0)
    scale = lax.rsqrt(jnp.mean(widened * widened, axis=1, keepdims=True) + 1e-06)
    return (widened * scale * gain[None, :]).astype(jnp.bfloat16)


def line_normalised(value, mirror, beside, facing, rows):
    width = value.shape[1]

    def kernel(at_ref, *refs):
        *block_refs, out_ref = refs
        at = at_ref[0]
        blocks = [ref[...].astype(jnp.float32) for ref in block_refs]
        squares = sum(jnp.sum(block[:rows] * block[:rows], axis=1, keepdims=True) for block in blocks)
        scale = lax.rsqrt(squares / (4 * width) + 1e-06)
        for block, away in zip(blocks, (0, 3, 1, 2)):
            gain = jnp.sum(block[rows:], axis=0, keepdims=True)
            where = pl.ds(pl.multiple_of((at ^ away) * width, width), width)
            out_ref[:, where] = (block[:rows] * scale * gain).astype(out_ref.dtype)

    return pl.pallas_call(
        kernel,
        out_shape=jax.ShapeDtypeStruct((rows, 4 * width), jnp.bfloat16),
        in_specs=[pl.BlockSpec(memory_space=pltpu.SMEM)]
        + [pl.BlockSpec(memory_space=pltpu.VMEM)] * 4,
        out_specs=pl.BlockSpec(memory_space=pltpu.VMEM),
        compiler_params=pltpu.CompilerParams(vmem_limit_bytes=16 * 1024 * 1024),
        cost_estimate=pl.CostEstimate(
            flops=16 * rows * width, bytes_accessed=16 * rows * width, transcendentals=rows
        ),
    )(lax.axis_index("col")[None], value, mirror, beside, facing)


def tie(*values):
    return lax.optimization_barrier(values)


def split_float(value, parts):
    pieces = []
    for _ in range(parts):
        piece = lax.reduce_precision(value, 8, 7)
        pieces.append(piece.astype(jnp.bfloat16))
        value = value - piece
    return pieces


def body(
    tokens,
    norm_gain,
    lengths,
    request_adapter,
    routes,
    route_weights,
    gate_weight,
    up_weight,
    down_weight,
    adapter_down,
    adapter_up,
):
    tok_rows, width_part = tokens.shape
    rows_axis, cols_axis = lax.axis_size("row"), lax.axis_size("col")
    row_at, col_at = lax.axis_index("row"), lax.axis_index("col")
    splits = rows_axis // EXPERTS
    chips = rows_axis // 2
    unit_gate, unit_up, unit_down = gate_weight[0], up_weight[0], down_weight[0]
    hidden_part = unit_gate.shape[0]
    line = cols_axis == 4

    gain_parts = jnp.stack(split_float(norm_gain, 3))
    sent = jnp.concatenate(
        [tokens, jnp.pad(gain_parts, ((0, GAIN_ROWS - 3), (0, 0)))], axis=0
    )
    hops = list(first_hops(sent, MIRROR, FACING)) if line else ring_gather(sent)

    local_adapters = adapter_down.shape[0]
    mine = jnp.concatenate([jnp.transpose(adapter_down, (0, 2, 1)), adapter_up], axis=0)
    mine = mine.reshape(2 * local_adapters * RANK, width_part)
    by_chip = [mine] + [row_xor(mine, by) for by in range(2, rows_axis - 2, 2)]
    if line:
        hops[0], mine = tie(hops[0], mine)
    by_chip.append(row_xor(mine, rows_axis - 2))
    assigned = routes.reshape(-1)
    assign_count = assigned.shape[0]
    expert_hot = (assigned[:, None] == jnp.arange(EXPERTS, dtype=jnp.int32)[None, :]).astype(
        jnp.bfloat16
    )
    earlier = (
        jnp.arange(assign_count, dtype=jnp.int32)[:, None]
        > jnp.arange(assign_count, dtype=jnp.int32)[None, :]
    ).astype(jnp.bfloat16)
    before = jnp.dot(earlier, expert_hot, preferred_element_type=jnp.float32)
    slot_index = jnp.sum(before * expert_hot.astype(jnp.float32), axis=1).astype(jnp.int32)
    placed_at = assigned * SLOTS + slot_index

    def placing(core, slots):
        place = jnp.arange(chips * slots, dtype=jnp.int32)
        target = row_at ^ (place // slots * 2 + core)
        wanted = (target // splits) * SLOTS + place % slots
        return (wanted[:, None] == placed_at[None, :]).astype(jnp.bfloat16)

    of_token = [
        jnp.sum(placing(core, SLOTS).reshape(-1, tok_rows, TOPK), axis=2) for core in (0, 1)
    ]
    if line:
        hops, of_token = tie(hops, of_token)
    if line:
        normed = line_normalised(sent, *hops, tok_rows)
    else:
        normed = normalised(side_by_side(sent, hops), tok_rows)
    normed, *by_chip[:-1] = tie(normed, *by_chip[:-1])

    def outgoing(core):
        placed = jnp.dot(of_token[core], normed, preferred_element_type=jnp.float32)
        return placed.astype(jnp.bfloat16).reshape(chips, SLOTS, D)

    there_half = outgoing(1)
    partner_own = row_xor(there_half[0], 1)
    partner_half = [partner_own] + list(row_xor(there_half[1:], 1))
    here_half = outgoing(0)

    groups = [[0], list(range(1, chips - 1)), [chips - 1]]
    pairs = [
        jnp.concatenate([here_half[offset], partner_half[offset]], axis=0)
        for offset in range(chips)
    ]
    if line:
        pairs[1], pairs[2], by_chip[-1] = tie(pairs[1], pairs[2], by_chip[-1])
    for offset in range(1, chips):
        if offset == chips - 1:
            pairs[1], pairs[-1] = tie(pairs[1], pairs[-1])
        pairs[offset] = row_xor(pairs[offset], 2 * offset)

    def hidden_of(offsets, earlier):
        arrived = jnp.concatenate(
            [
                pairs[offset][first : first + CAP]
                for offset in offsets
                for first in (0, SLOTS)
            ],
            axis=0,
        )
        arrived, *earlier = tie(arrived, *earlier)
        gate_sum = contract_last(arrived, unit_gate)
        up_sum = contract_last(arrived, unit_up)
        value = (jax.nn.silu(gate_sum) * up_sum).astype(jnp.bfloat16)
        return value, earlier

    def first_of(value, *pairs_of):
        return list(first_hops(value, *pairs_of)) if line else ring_gather(value)

    value, _ = hidden_of(groups[0], [])
    hidden, hops = [value], [first_of(value, MIRROR, OVER)]

    hidden[0], pairs[1:-1], by_chip = tie(hidden[0], pairs[1:-1], by_chip)
    factors = both_cores(jnp.stack(by_chip))
    factors = factors.reshape(rows_axis, 2, local_adapters * RANK, width_part)
    down_rows = factors[:, 0].reshape(-1, width_part)
    up_rows = factors[:, 1].reshape(-1, width_part)
    normed, pairs[1:-1] = tie(normed, pairs[1:-1])
    own = lax.dynamic_slice(normed, (0, col_at * width_part), (tok_rows, width_part))
    req_ends = jnp.cumsum(lengths)
    position = row_at * tok_rows + jnp.arange(tok_rows, dtype=jnp.int32)
    request = jnp.sum((position[None, :] >= req_ends[:, None]).astype(jnp.int32), axis=0)
    request_hot = request[None, :] == jnp.arange(lengths.shape[0], dtype=jnp.int32)[:, None]
    adapter = jnp.sum(jnp.where(request_hot, request_adapter[:, None], 0), axis=0)
    adapter_count = local_adapters * rows_axis
    order = jnp.arange(adapter_count, dtype=jnp.int32)
    held = (row_at ^ (order // local_adapters)) * local_adapters + order % local_adapters
    select = held[:, None] == adapter[None, :]
    projected = contract_last(down_rows, own).reshape(adapter_count, RANK, tok_rows)
    partial_low = jnp.sum(jnp.where(select[:, None, :], projected, 0.0), axis=0)
    extra = jnp.zeros((0, hidden_part), jnp.bfloat16)
    if line:
        pieces = [piece[at : at + 8] for piece in split_float(partial_low, 2) for at in (0, 8)]
        spare = (0, LOW_STRIDE - tok_rows)
        extra = jnp.concatenate([jnp.pad(piece, ((0, 0), spare)) for piece in pieces], axis=1)
        extra = jnp.pad(extra, ((0, 0), (0, hidden_part - extra.shape[1])))

    if line:
        hops[0][0], extra = tie(hops[0][0], extra)
    passed = along(hops[0][0], OUTWARD) if line else None
    value, (extra, *hops[0][:2]) = hidden_of(groups[1], [extra] + hops[0][:2])
    hidden.append(jnp.concatenate([value, extra], axis=0))
    hops.append(first_of(hidden[1], ACROSS, OVER))
    earlier = hops[0][1:] + [passed] if line else []
    pairs[-1], hidden[1] = tie(pairs[-1], hidden[1])
    value, (hidden[1], *earlier) = hidden_of(groups[2], [hidden[1]] + earlier)
    hidden.append(value)
    hops.append(first_of(value, MIRROR, OVER))
    if line:
        beside, over, passed = earlier
        hops[0] = [hops[0][0], beside, over + passed]

    def whole_of(number):
        return (in_line if line else side_by_side)(
            hidden[number], *(hops[number] if line else [hops[number]])
        )

    def block_sum(whole):
        return jnp.dot(whole, unit_down, preferred_element_type=jnp.float32)

    late_weights, hidden[2] = tie(route_weights, hidden[2])

    def weights_at(core):
        place = jnp.arange(chips * CAP, dtype=jnp.int32)
        target = row_at ^ (place // CAP * 2 + core)
        wanted = (target // splits) * SLOTS + place % CAP
        at = wanted[:, None, None] == placed_at.reshape(1, tok_rows, TOPK)
        return split_float(jnp.sum(jnp.where(at, late_weights[None], 0.0), axis=2), 2)

    place_weights = [weights_at(core) for core in (0, 1)]

    def weighted(core_blocks):
        return sum(
            lax.dot_general(
                part[first : first + rows.shape[0]],
                rows,
                (((0,), (0,)), ((), ())),
                preferred_element_type=jnp.float32,
            )
            for parts, (first, rows) in zip(place_weights, core_blocks)
            for part in parts
        )

    out = block_sum(whole_of(0)).astype(jnp.bfloat16)
    returned = [out]
    if line:
        mirror, beside, over = hops[1]
        mirror, hidden[2], returned[0], late_down = tie(mirror, hidden[2], out, unit_down)
        near = along(mirror, OUTWARD)
        beside, mirror = tie(beside, mirror)
        over, beside = tie(over, beside)
        hops[1] = [mirror + along(over, OUTWARD), beside, over + near]
        hops[2][0], over = tie(hops[2][0], over)
        hops[1][2] = over + near
        passed = along(hops[2][0], OUTWARD)
    whole = whole_of(1)
    count = len(groups[1]) * 2 * CAP
    out = block_sum(whole[:count]).astype(jnp.bfloat16)
    for index, offset in enumerate(groups[1]):
        returned.append(row_xor(out[index * 2 * CAP : (index + 1) * 2 * CAP], 2 * offset))
    if line:
        rest = whole[count:].reshape(8, cols_axis, hidden_part)[:, :, : 4 * LOW_STRIDE]
        rest = jnp.sum(rest.astype(jnp.float32), axis=1)
        rest = jnp.sum(rest.reshape(8, 2, 2, LOW_STRIDE), axis=1)[:, :, :tok_rows]
        low_sum = jnp.concatenate([rest[:, 0], rest[:, 1]], axis=0)
    else:
        low_sum = col_sum(partial_low)
    low_rank = low_sum.astype(jnp.bfloat16)
    expanded = jnp.where(select[:, None, :], low_rank[None], 0).reshape(
        adapter_count * RANK, tok_rows
    )
    branch = lax.dot_general(
        expanded, up_rows, (((0,), (0,)), ((), ())), preferred_element_type=jnp.float32
    )
    if line:
        mirror, beside, facing = hops[2]
        part = block_sum(in_line(hidden[2], mirror, beside, jnp.zeros_like(mirror)))
        facing_down = lax.dynamic_slice(
            late_down, ((col_at ^ 2) * hidden_part, 0), (hidden_part, width_part)
        )
        facing, passed, branch, part, facing_down = tie(
            facing, passed, branch, part, facing_down
        )
        out = part + jnp.dot(facing + passed, facing_down, preferred_element_type=jnp.float32)
    else:
        out = block_sum(whole_of(2))
    out = out.astype(jnp.bfloat16)
    returned.append(row_xor(out, 2 * chips - 2))
    near = jnp.stack(returned)
    near_others = row_xor(near[:, CAP:], 1)
    near = [near[:, :CAP].reshape(-1, width_part), near_others.reshape(-1, width_part)]
    mixed = branch + weighted([(0, rows) for rows in near])
    return mixed.astype(jnp.bfloat16)


def solution(mesh):
    in_specs = (
        P("row", "col"),
        P("col"),
        P(),
        P(),
        P("row", None),
        P("row", None),
        P("row", "col", None),
        P("row", "col", None),
        P("row", None, "col"),
        P("row", "col", None),
        P("row", None, "col"),
    )
    out_specs = P("row", "col")
    return jax.shard_map(body, mesh=mesh, in_specs=in_specs, out_specs=out_specs, check_vma=False)
```
